128 devices in a mesh: ctx: 16 (over x_hi, y, core), exp: 8 (over x_lo, z).
Axes of the slice: x: 4 (x_hi: 2, x_lo: 2; x = x_hi * 2 + x_lo), y: 4, z: 4, core: 2. Of those that a mesh axis runs over, the one named last changes fastest.
Arguments:
- queries: bfloat16 [2048, 6144], P('ctx', 'exp'), may hold values from -96 to 96, as said below
- k_load: bfloat16 [2048, 1024], P('ctx', 'exp'), may hold values from -4 to 4
- v_load: bfloat16 [2048, 1024], P('ctx', 'exp'), may hold values from -5 to 5
- kv_scale: bfloat16 [128, 8, 2], P('ctx', 'exp'), may hold values from 0.5 to 2
- doc_ids: int32 [2048], P('ctx'), may hold values from 0 to 1, as said below
- residual_in: bfloat16 [2048, 6144], P(('ctx', 'exp')), may hold values from -3 to 3
- out_weight: bfloat16 [6144, 6144], P('exp', 'ctx'), may hold values from -0.15625 to 0.15625
- norm_gain: bfloat16 [6144], replicated, may hold values from 0.099609375 to 1.8984375
- w_gate: bfloat16 [8, 6144, 8192], P('exp', None, 'ctx'), may hold values from -0.078125 to 0.078125
- w_up: bfloat16 [8, 6144, 8192], P('exp', None, 'ctx'), may hold values from -0.078125 to 0.078125
- w_down: bfloat16 [8, 8192, 6144], P('exp', 'ctx'), may hold values from -0.125 to 0.125
- expert_ids: int32 [2048, 2], P(('ctx', 'exp')), may hold values from 0 to 7, all different within a row; in each aligned block of 16 rows (0 to 15, 16 to 31, ...) at most 8 rows name the same one
- route_logit: float32 [2048, 2], P(('ctx', 'exp')), may hold values from -6 to 6
Outputs:
- mixed: bfloat16 [2048, 6144], P(('ctx', 'exp'))
The draws below stay inside these ranges and needn't reach their ends.
Inputs may be any that keep to these rules, and one draw needn't show every extreme that they name: `queries`: some rows may have every head equal to a multiple of its key head's row of k_load at the same token. `doc_ids`: never falling along the tokens. `expert_ids`: each row names two different experts; in each aligned block of 16 rows (the rows of one device) no expert is named by more than 8 rows, a bound that some block reaches.
All inputs are finite; a program needn't handle non-finite values.
Results may differ from the reference program's by a relative error of at most 0.03.
Values may be sent and summed in bfloat16 or wider, within the bound.
No kernel may reach another device: no remote copies, remote signals or barrier semaphores. Data moves between devices by JAX's collectives and lax.ppermute only.
A program may use at most 128 MiB of HBM per device.

```python
import math
import jax
import jax.numpy as jnp
import numpy as np
from jax import lax

D = 6144
HQ = 48
KVH = 8
HD = 128
FH = 8192
KBLK = 16
TOP = 2
TOKENS = 2048
ROWS_DEV = 16
EXPERTS = 8
CAP = 8
HSLICE = 512
N_CTX = 16


def key_base(key):
    return jax.random.truncated_normal(key, -4.0, 4.0, (TOKENS, KVH * HD), jnp.float32)


def draw_k_load(key, part):
    base = key_base(key)
    return base.astype(jnp.bfloat16)


def draw_queries(key, part):
    key = jax.random.fold_in(key, 5)
    drawn = jax.random.truncated_normal(key, -4.0, 4.0, (TOKENS, HQ * HD), jnp.float32)
    return drawn.astype(jnp.bfloat16)


def draw_doc_ids(key, part):
    key = jax.random.fold_in(key, 11)
    reach = TOKENS // 8
    move = jax.random.randint(key, (1,), -reach, reach + 1, jnp.int32)
    cut = 3 * (TOKENS // 4) + move
    position = jnp.arange(TOKENS, dtype=jnp.int32)
    return (position >= cut[0]).astype(jnp.int32)


def block_scale(key, dims, pieces, low, high):
    gain = 1.0
    for dim, shards_of in pieces:
        heights = jax.random.uniform(jax.random.fold_in(jax.random.fold_in(key, 6), dim), (shards_of,), jnp.float32, low / len(pieces), high / len(pieces))
        gain = gain * jnp.repeat(jnp.exp(heights), dims[dim] // shards_of).reshape((-1,) + (1,) * (len(dims) - 1 - dim))
    return gain


def deal_out(rng, own, number, rows, amount, top, limit, slope):
    order = jax.random.permutation(rng, amount)
    heavy_load, ordinary = load_shares(amount, rows * top, limit, slope, True), load_shares(amount, rows * top, limit, slope, False)
    places = jnp.arange(amount)

    def named(tallies, rotation):
        used = int((tallies > 0).sum())
        fixed = max(1, used // 4)
        passed = fixed + (places - fixed + rotation * (used - fixed)) % max(1, amount - fixed)
        return jnp.zeros((amount,), jnp.int32).at[order[jnp.where(places < fixed, places, passed)]].set(jnp.asarray(tallies, jnp.int32))

    tallies = jnp.where(number % 4 == 0, named(heavy_load, number // 4), named(ordinary, number - number // 4 - 1))
    mixed = jax.random.permutation(jax.random.fold_in(own, 3), amount)
    giver, receiver = mixed[0:amount // 2 * 2:2], mixed[1:amount // 2 * 2:2]
    slack = jnp.minimum(tallies[giver] - 1, limit - tallies[receiver]) // 2
    slack = jnp.where((giver == order[0]) | (receiver == order[0]) | (tallies[receiver] == 0), 0, jnp.maximum(slack, 0))
    passed = jax.random.randint(jax.random.fold_in(own, 4), (amount // 2,), 0, 1 << 20) % (slack + 1)
    tallies = tallies.at[giver].add(-passed).at[receiver].add(passed)
    labels = jnp.searchsorted(jnp.cumsum(tallies), jnp.arange(rows * top), side="right").astype(jnp.int32)
    table = labels.reshape(top, rows).T
    table = table[jax.random.permutation(jax.random.fold_in(own, 1), rows)]
    rotation = jax.random.randint(jax.random.fold_in(own, 2), (rows, 1), 0, top)
    return jnp.take_along_axis(table, (jnp.arange(top)[None, :] + rotation) % top, axis=1)


def load_shares(count, total, most, slope, full):
    loads = [(1 << 20) // math.isqrt(rank ** slope) + 1 for rank in range(1, count + 1)]
    largest = most if full else min(most, max(-(-total // count), total * loads[0] // sum(loads)))
    least = 1 if total - largest >= count - 1 else 0
    holding, spare = [largest] + [least] * (count - 1), total - largest - least * (count - 1)
    while spare > 0:
        free = [i for i in range(1, count) if holding[i] < largest] or [i for i in range(1, count) if holding[i] < most]
        whole, remaining = sum([loads[i] for i in free]), spare
        for i in free:
            addition = min(most - holding[i], max(1, remaining * loads[i] // whole), spare)
            holding[i] = holding[i] + addition
            spare = spare - addition
    return np.array(holding)


def noise(stream_key, shape, scale, most, cuts=(), kind=jnp.bfloat16):
    values = scale * jax.random.normal(stream_key, shape, jnp.float32)
    if cuts:
        values = values * block_scale(stream_key, shape, cuts, -0.22, 0.18)
    return jnp.clip(values, -most, most).astype(kind)


def setup_inputs(seed: int = 0) -> dict:
    streams_of = jax.random.split(jax.random.key(seed), 14)
    queries = draw_queries(jax.random.fold_in(streams_of[13], 71), 0)
    k_load = draw_k_load(jax.random.fold_in(streams_of[13], 71), 0)
    v_load = noise(streams_of[2], (TOKENS, KVH * HD), 1.0, 5.0, ((0, 16), (1, 8)))
    kv_scale = jnp.clip(jnp.exp(math.log(2.0) - 1.3862944 * jax.random.uniform(streams_of[3], (TOKENS // KBLK, KVH, 2), jnp.float32) ** block_scale(streams_of[3], (TOKENS // KBLK, KVH, 2), ((0, 16), (1, 8)), -0.2, 0.2)), 0.5, 2.0).astype(jnp.bfloat16)
    doc_ids = draw_doc_ids(jax.random.fold_in(streams_of[13], 71), 0)
    residual_in = noise(streams_of[5], (TOKENS, D), 0.5, 3.0, ((0, 128),))
    out_weight = noise(streams_of[6], (HQ * HD, D), (HQ * HD // 4) ** -0.5, 0.15625, ((0, 8), (1, 16)))
    norm_gain = jnp.clip(1.0 + 0.18 * jax.random.normal(streams_of[7], (D,), jnp.float32), 0.099609375, 1.8984375).astype(jnp.bfloat16)
    w_gate = noise(streams_of[8], (EXPERTS, D, FH), D ** -0.5, 0.078125, ((0, 8), (2, 16)))
    w_up = noise(streams_of[9], (EXPERTS, D, FH), D ** -0.5, 0.078125, ((0, 8), (2, 16)))
    w_down = noise(streams_of[10], (EXPERTS, FH, D), (FH // 4) ** -0.5, 0.125, ((0, 8), (1, 16)))
    expert_ids_keys = jax.random.split(jax.random.fold_in(streams_of[11], 1), TOKENS // ROWS_DEV)
    expert_ids_turns = jax.random.permutation(jax.random.fold_in(streams_of[11], 3), TOKENS // ROWS_DEV)
    expert_ids = jax.vmap(lambda own, number: deal_out(jax.random.fold_in(streams_of[11], 2), own, number, ROWS_DEV, EXPERTS, 2, CAP, 2))(expert_ids_keys, expert_ids_turns).reshape((TOKENS, TOP))
    route_logit = noise(streams_of[12], (TOKENS, TOP), 1.5, 6.0, ((0, 128),), jnp.float32)
    return dict(queries=queries, k_load=k_load, v_load=v_load, kv_scale=kv_scale, doc_ids=doc_ids, residual_in=residual_in, out_weight=out_weight, norm_gain=norm_gain, w_gate=w_gate, w_up=w_up, w_down=w_down, expert_ids=expert_ids, route_logit=route_logit)


def dequantize(payload, scales, which):
    factor = jnp.repeat(scales[:, :, which].astype(jnp.float32), KBLK, axis=0)
    shaped = payload.astype(jnp.float32).reshape(payload.shape[0], KVH, HD)
    return (shaped * factor[:, :, None]).astype(jnp.bfloat16)

def add_group(running, pair):
    partial_sum = jnp.dot(pair[0], pair[1], preferred_element_type=jnp.float32)
    rounded = lax.optimization_barrier(partial_sum.astype(jnp.bfloat16))
    return (running + rounded.astype(jnp.float32), None)

def reference(queries, k_load, v_load, kv_scale, doc_ids, residual_in, out_weight, norm_gain, w_gate, w_up, w_down, expert_ids, route_logit):
    keys = dequantize(k_load, kv_scale, 0)
    values = dequantize(v_load, kv_scale, 1)
    position = jnp.arange(TOKENS, dtype=jnp.int32)
    allowed = (position[:, None] >= position[None, :]) & (doc_ids[:, None] == doc_ids[None, :])
    query_heads = queries.reshape(TOKENS, HQ, HD)
    group_size = HQ // KVH

    def one_head(head):
        kv_head = head // group_size
        query = lax.dynamic_index_in_dim(query_heads, head, 1, keepdims=False)
        key_rows = lax.dynamic_index_in_dim(keys, kv_head, 1, keepdims=False)
        value_rows = lax.dynamic_index_in_dim(values, kv_head, 1, keepdims=False)
        scores = jnp.dot(query, key_rows.T, preferred_element_type=jnp.float32) / math.sqrt(HD)
        scores = jnp.where(allowed, scores, -1e+30)
        best = lax.optimization_barrier(jnp.max(scores, axis=1, keepdims=True))
        expo = jnp.where(allowed, jnp.exp(scores - best), 0.0)
        total = lax.optimization_barrier(jnp.sum(expo, axis=1, keepdims=True))
        weighted = jnp.dot(expo.astype(jnp.bfloat16), value_rows, preferred_element_type=jnp.float32) / total
        return weighted.astype(jnp.bfloat16)
    heads_out = lax.map(one_head, jnp.arange(HQ, dtype=jnp.int32))
    attn = jnp.transpose(heads_out, (1, 0, 2)).reshape(TOKENS, HQ * HD)
    resid = (residual_in.astype(jnp.float32) + jnp.dot(attn, out_weight, preferred_element_type=jnp.float32)).astype(jnp.bfloat16)
    wide = resid.astype(jnp.float32)
    normed = (wide * lax.rsqrt(lax.optimization_barrier(jnp.mean(wide * wide, axis=1, keepdims=True)) + 1e-05) * norm_gain.astype(jnp.float32)).astype(jnp.bfloat16)
    route = jax.nn.softmax(route_logit.astype(jnp.float32), axis=1).reshape(-1)
    flat_ids = expert_ids.reshape(-1)
    flat_rows = jnp.arange(TOKENS * TOP, dtype=jnp.int32) // TOP
    most_rows = TOKENS // ROWS_DEV * CAP
    running = wide
    for expert in range(EXPERTS):
        order = jnp.argsort((flat_ids != expert).astype(jnp.int32), stable=True)[:most_rows]
        chosen = flat_ids[order] == expert
        token_rows = flat_rows[order]
        picked = normed[token_rows]
        gate = jnp.dot(picked, w_gate[expert], preferred_element_type=jnp.float32)
        upward = jnp.dot(picked, w_up[expert], preferred_element_type=jnp.float32)
        hidden = (jax.nn.silu(gate) * upward).astype(jnp.bfloat16)
        hidden_groups = jnp.transpose(hidden.reshape(most_rows, N_CTX, HSLICE), (1, 0, 2))
        down_groups = w_down[expert].reshape(N_CTX, HSLICE, D)
        start_sum = jnp.zeros((most_rows, D), jnp.float32)
        expert_out = lax.scan(add_group, start_sum, (hidden_groups, down_groups))[0].astype(jnp.bfloat16)
        scale_rows = jnp.where(chosen, route[order], 0.0)
        running = running.at[token_rows].add(expert_out.astype(jnp.float32) * scale_rows[:, None])
    return running.astype(jnp.bfloat16)
```

```python
import math

import jax
import jax.numpy as jnp
from jax import lax
from jax.sharding import PartitionSpec as P

HQ = 48
KVH = 8
HD = 128
KBLK = 16
TOP = 2
CAP = 8
NY = 4
NE = 8
BOTH = ("ctx", "exp")
F32 = jnp.float32
BF16 = jnp.bfloat16


def partner(flip_x=0, step_y=0, flip_core=0):
    pairs = []
    for source in range(128):
        ctx, exp = divmod(source, NE)
        x_hi, y, core = ctx // 8, (ctx // 2) % NY, ctx % 2
        target = ((x_hi ^ flip_x) * 8 + ((y + step_y) % NY) * 2 + (core ^ flip_core)) * NE + exp
        pairs.append((source, target))
    return pairs


def flip_x(value):
    return lax.ppermute(value, BOTH, partner(flip_x=1))


def flip_core(value):
    return lax.ppermute(value, BOTH, partner(flip_core=1))


def from_y(value, step):
    return lax.ppermute(value, BOTH, partner(step_y=-step))


def dequantize(payload, scales, which):
    factor = jnp.repeat(scales[:, 0, which].astype(F32), KBLK, axis=0)
    return (payload.astype(F32) * factor[:, None]).astype(BF16)


def slots_of(ids):
    order = jnp.arange(ids.shape[0], dtype=jnp.int32)
    same = (ids[:, None] == ids[None, :]) & (order[None, :] < order[:, None])
    return jnp.sum(same.astype(jnp.int32), axis=1)


def gather_y(own, axis):
    half = own.shape[axis] // 2
    above = from_y(own, 1)
    below = from_y(own, -1)
    far_lo = from_y(lax.slice_in_dim(below, 0, half, axis=axis), -1)
    far_hi = from_y(lax.slice_in_dim(above, half, 2 * half, axis=axis), 1)
    far = lax.concatenate([far_lo, far_hi], axis)
    return own, above, below, far


STEPS = (0, 1, -1, 2)


def attention(queries, key_value, doc_ids, place):
    x_hi, y, core = place
    tok = queries.shape[0]
    own, own_docs = key_value, doc_ids
    shards = [own]
    for step in (1, -1, 2):
        shards.append(from_y(own, step))
    across = flip_x(own)
    shards.append(across)
    for step in (1, -1, 2):
        shards.append(from_y(across, step))
    mine = jnp.stack(shards)
    other = flip_core(mine)
    both = jnp.stack([mine, other])
    start = []
    for c in (core, 1 - core):
        for xh in (x_hi, 1 - x_hi):
            for step in STEPS:
                start.append(((xh * NY + (y + step) % NY) * 2 + c) * tok)
    start = jnp.stack(start)
    both = both.reshape(16, tok + 16, 256)
    keys = both[:, :tok, :128].reshape(16 * tok, HD)
    values = both[:, :tok, 128:].reshape(16 * tok, HD)
    docs = both[:, tok, :128].reshape(16 * tok)
    key_pos = (start[:, None] + jnp.arange(tok, dtype=jnp.int32)[None, :]).reshape(-1)
    query_pos = start[0] + jnp.arange(tok, dtype=jnp.int32)
    allowed = (query_pos[:, None] >= key_pos[None, :]) & (
        own_docs.astype(BF16)[:, None] == docs[None, :]
    )
    heads = queries.reshape(tok, -1, HD)
    scores = jnp.einsum("tqd,sd->qts", heads, keys, preferred_element_type=F32)
    scores = jnp.where(allowed, scores * (1.0 / math.sqrt(HD)), -1e30)
    best = jnp.max(scores, axis=2, keepdims=True)
    expo = jnp.where(allowed, jnp.exp(scores - best), 0.0)
    total = jnp.sum(expo, axis=2)
    accum = jnp.einsum("qts,sd->qtd", expo.astype(BF16), values, preferred_element_type=F32)
    out = (accum / total[..., None]).astype(BF16)
    across_ids = across[tok + 1, : 16 * TOP].astype(jnp.int32)
    return jnp.transpose(out, (1, 0, 2)).reshape(tok, -1), across_ids


def per_device(
    queries,
    k_load,
    v_load,
    kv_scale,
    doc_ids,
    residual_in,
    out_weight,
    norm_gain,
    w_gate,
    w_up,
    w_down,
    expert_ids,
    route_logit,
):
    ctx = lax.axis_index("ctx")
    x_hi, y, core = ctx // 8, (ctx // 2) % NY, ctx % 2
    tok = queries.shape[0]
    rows = residual_in.shape[0]
    width = residual_in.shape[1]
    half = width // 2
    gate_own, up_own, down_own = w_gate[0], w_up[0], w_down[0]

    ids = expert_ids.reshape(-1)
    info = jnp.concatenate(
        [doc_ids.astype(BF16), ids.astype(BF16), jnp.zeros((256 - tok - rows * TOP,), BF16)]
    )
    key_value = jnp.concatenate(
        [
            jnp.concatenate([dequantize(k_load, kv_scale, 0), dequantize(v_load, kv_scale, 1)], 1),
            jnp.pad(info.reshape(2, 128), ((0, 14), (0, 128))),
        ],
        0,
    )
    attn, across_ids = attention(queries, key_value, doc_ids, (x_hi, y, core))

    proj_mine = jnp.concatenate(gather_y(out_weight, 0), 1)
    proj_other = flip_core(proj_mine)
    attn_across = flip_x(attn)
    paired = jnp.stack([attn.reshape(NE, rows, -1), attn_across.reshape(NE, rows, -1)], 1)
    paired = paired.reshape(2 * tok, -1)
    partial = jnp.concatenate(
        [
            jnp.dot(paired, proj_mine, preferred_element_type=F32).astype(BF16),
            jnp.dot(paired, proj_other, preferred_element_type=F32).astype(BF16),
        ],
        1,
    )
    terms = lax.all_to_all(
        partial.reshape(NE, 2 * rows, half), "exp", split_axis=0, concat_axis=0, tiled=True
    )
    summed = jnp.sum(terms.astype(F32), axis=0)
    summed = summed.reshape(2 * rows, 2, NY, half // 8)
    ring = jnp.stack([summed[:, :, 0], summed[:, :, 1], summed[:, :, 3], summed[:, :, 2]], 2)
    ring = lax.dynamic_slice_in_dim(jnp.concatenate([ring, ring], 2), (NY - y) % NY, NY, 2)
    ring = jnp.where(core == 0, ring, ring[:, ::-1])
    attn_rows = jnp.transpose(ring, (0, 2, 1, 3)).reshape(2 * rows, half)
    res_own = lax.dynamic_slice_in_dim(residual_in, x_hi * half, half, 1)
    res_send = lax.dynamic_slice_in_dim(residual_in, (1 - x_hi) * half, half, 1)
    res_cols = jnp.concatenate([res_own, flip_x(res_send)], 0)
    resid = (res_cols.astype(F32) + attn_rows).astype(BF16)

    slots_own = slots_of(ids)
    slots_across = slots_of(across_ids)
    place = jnp.concatenate(
        [
            (ids * 2 + x_hi) * CAP + slots_own,
            (across_ids * 2 + 1 - x_hi) * CAP + slots_across,
        ]
    ).reshape(2 * rows, TOP)
    row_no = jnp.arange(NE * 2 * CAP, dtype=jnp.int32)[:, None]
    dispatch = ((row_no == place[None, :, 0]) | (row_no == place[None, :, 1])).astype(BF16)
    outgoing = jnp.dot(dispatch, resid, preferred_element_type=F32).astype(BF16)
    arrived = lax.all_to_all(
        outgoing.reshape(NE, 2 * CAP, half), "exp", split_axis=0, concat_axis=0, tiled=True
    ).reshape(NE * 2 * CAP, half)

    gate_other, up_other, down_other = flip_core(gate_own), flip_core(up_own), flip_core(down_own)

    near, above, below, far = gather_y(arrived, 0)
    near_x = flip_x(near)
    above_x, below_x = from_y(near_x, 1), from_y(near_x, -1)
    far_x = flip_x(far)
    resid_across = flip_x(resid[rows:])
    parts = ((x_hi, [near, above, below, far]), (1 - x_hi, [near_x, above_x, below_x, far_x]))
    square, products = 0.0, None
    for which, blocks in parts:
        block = jnp.concatenate(blocks, 0).astype(F32)
        square = square + jnp.sum(block * block, axis=1, keepdims=True)
        gain = lax.dynamic_slice_in_dim(norm_gain, which * half, half, 0).astype(F32)
        scaled = (block * gain[None, :]).astype(BF16)
        fresh = [
            jnp.dot(
                scaled,
                lax.dynamic_slice_in_dim(weight, which * half, half, 0),
                preferred_element_type=F32,
            )
            for weight in (gate_own, gate_other, up_own, up_other)
        ]
        products = fresh if products is None else [a + b for a, b in zip(products, fresh)]
    scale = lax.rsqrt(square / width + 1e-05)
    hidden = [
        (jax.nn.silu(products[i] * scale) * (products[2 + i] * scale)).astype(BF16)
        for i in range(2)
    ]

    split = [h.reshape(NY, NE, 2, CAP, -1) for h in hidden]

    def pick(h, which):
        taken = jnp.where(which == 0, h[:, :, 0], h[:, :, 1])
        return taken.reshape(NY, NE * CAP, -1)

    mine = [pick(h, x_hi) for h in split]
    theirs = [pick(h, 1 - x_hi) for h in split]

    def down(blocks):
        total = jnp.dot(
            jnp.concatenate([b[0] for b in blocks], 0), down_own, preferred_element_type=F32
        ) + jnp.dot(
            jnp.concatenate([b[1] for b in blocks], 0), down_other, preferred_element_type=F32
        )
        return total.reshape(len(blocks), NE * CAP, width)

    def block(source, i):
        return (source[0][i], source[1][i])

    first = down([block(theirs, 1), block(theirs, 2), block(theirs, 3)]).astype(BF16)
    from_below = from_y(first[0], -1)
    from_above = from_y(first[1], 1)
    from_far = flip_x(first[2])
    second = down([block(theirs, 0), block(mine, 3)])
    cross = (second[0] + from_below.astype(F32) + from_above.astype(F32)).astype(BF16)
    far_sum = (second[1] + from_far.astype(F32)).astype(BF16)
    from_cross = flip_x(cross)
    far_lo = from_y(far_sum[:, :half], -1)
    far_hi = from_y(far_sum[:, half:], 1)
    third = down([block(mine, 1), block(mine, 2), block(mine, 0)])
    to_above = jnp.concatenate([third[0][:, :half] + far_lo.astype(F32), third[0][:, half:]], 1)
    to_below = jnp.concatenate([third[1][:, :half], third[1][:, half:] + far_hi.astype(F32)], 1)
    last_below = from_y(to_above.astype(BF16), -1)
    last_above = from_y(to_below.astype(BF16), 1)
    expert_out = (
        third[2] + from_cross.astype(F32) + last_below.astype(F32) + last_above.astype(F32)
    ).astype(BF16)

    returned = lax.all_to_all(
        expert_out.reshape(NE, CAP, width), "exp", split_axis=0, concat_axis=0, tiled=True
    ).reshape(NE * CAP, width)
    route = jax.nn.softmax(route_logit, axis=1)
    position = (ids * CAP + slots_own).reshape(rows, TOP)
    column = jnp.arange(NE * CAP, dtype=jnp.int32)[None, :]
    halves = [resid[:rows], resid_across]
    own_row = jnp.where(
        x_hi == 0, jnp.concatenate(halves, 1), jnp.concatenate(halves[::-1], 1)
    ).astype(F32)
    for k in range(TOP):
        chosen = (position[:, k : k + 1] == column).astype(BF16)
        own_row = own_row + route[:, k : k + 1] * jnp.dot(
            chosen, returned, preferred_element_type=F32
        )
    return own_row.astype(BF16)


def solution(mesh):
    return jax.shard_map(
        per_device,
        mesh=mesh,
        in_specs=(
            P("ctx", "exp"),
            P("ctx", "exp"),
            P("ctx", "exp"),
            P("ctx", "exp", None),
            P("ctx"),
            P(("ctx", "exp"), None),
            P("exp", "ctx"),
            P(),
            P("exp", None, "ctx"),
            P("exp", None, "ctx"),
            P("exp", "ctx", None),
            P(("ctx", "exp"), None),
            P(("ctx", "exp"), None),
        ),
        out_specs=P(("ctx", "exp"), None),
        check_vma=False,
    )
```

```python
import functools
import math

import jax
import jax.numpy as jnp
from jax import lax
from jax.experimental import pallas as pl
from jax.experimental.pallas import tpu as pltpu
from jax.sharding import PartitionSpec as P

HQ = 48
KVH = 8
HD = 128
KBLK = 16
TOP = 2
CAP = 8
NY = 4
NE = 8
BOTH = ("ctx", "exp")
F32 = jnp.float32
BF16 = jnp.bfloat16


def partner(flip_x=0, step_y=0, flip_core=0):
    pairs = []
    for source in range(128):
        ctx, exp = divmod(source, NE)
        x_hi, y, core = ctx // 8, (ctx // 2) % NY, ctx % 2
        target = ((x_hi ^ flip_x) * 8 + ((y + step_y) % NY) * 2 + (core ^ flip_core)) * NE + exp
        pairs.append((source, target))
    return pairs


def flip_x(value):
    return lax.ppermute(value, BOTH, partner(flip_x=1))


def flip_core(value):
    return lax.ppermute(value, BOTH, partner(flip_core=1))


def from_y(value, step):
    return lax.ppermute(value, BOTH, partner(step_y=-step))


def slots_of(ids):
    order = jnp.arange(ids.shape[0], dtype=jnp.int32)
    same = (ids[:, None] == ids[None, :]) & (order[None, :] < order[:, None])
    return jnp.sum(same.astype(jnp.int32), axis=1)


def gather_y(own, axis):
    half = own.shape[axis] // 2
    above = from_y(own, 1)
    below = from_y(own, -1)
    far_lo = from_y(lax.slice_in_dim(below, 0, half, axis=axis), -1)
    far_hi = from_y(lax.slice_in_dim(above, half, 2 * half, axis=axis), 1)
    far = lax.concatenate([far_lo, far_hi], axis)
    return own, above, below, far


STEPS = (0, 1, -1, 2)
INNER = 2
OUTER = 4


def pack(k_load, v_load, scales, docs, out, keys, values, sems):
    copies = [
        pltpu.make_async_copy(k_load, keys, sems.at[0]),
        pltpu.make_async_copy(v_load, values, sems.at[1]),
    ]
    for copy in copies:
        copy.start()
    tok = keys.shape[0]
    block = lax.broadcasted_iota(jnp.int32, (tok, tok // KBLK), 0) // KBLK
    group = lax.broadcasted_iota(jnp.int32, (tok, tok // KBLK), 1)
    picked = jnp.where(block == group, 1.0, 0.0).astype(BF16)
    factor = lax.dot_general(
        picked, scales[...], (((1,), (1,)), ((), ())), preferred_element_type=F32
    )
    wide = jnp.broadcast_to(docs[...].astype(F32), (16, tok)).astype(BF16)
    out[tok:, :HD] = wide
    out[tok:, HD:] = wide
    copies[0].wait()
    out[:tok, :HD] = (keys[...].astype(F32) * factor[:, 0:1]).astype(BF16)
    copies[1].wait()
    out[:tok, HD:] = (values[...].astype(F32) * factor[:, 1:2]).astype(BF16)


def packed_keys(k_load, v_load, kv_scale, doc_ids):
    vmem, hbm = pl.BlockSpec(memory_space=pltpu.VMEM), pl.BlockSpec(memory_space=pl.ANY)
    tok = k_load.shape[0]
    return pl.pallas_call(
        pack,
        out_shape=jax.ShapeDtypeStruct((tok + 16, 2 * HD), BF16),
        in_specs=[hbm, hbm, vmem, vmem],
        out_specs=vmem,
        scratch_shapes=[
            pltpu.VMEM(k_load.shape, BF16),
            pltpu.VMEM(v_load.shape, BF16),
            pltpu.SemaphoreType.DMA((2,)),
        ],
        compiler_params=pltpu.CompilerParams(vmem_limit_bytes=8 * 2**20),
        cost_estimate=pl.CostEstimate(flops=200000, bytes_accessed=200000, transcendentals=0),
    )(k_load, v_load, kv_scale[:, 0, :].T, doc_ids[None, :])


def attend(start, queries, mine, other, out, scores):
    tok = queries.shape[0]
    heads = queries.shape[1] // HD
    stacked = jnp.concatenate([queries[:, i * HD : (i + 1) * HD] for i in range(heads)], 0)
    shards = [(mine, i) for i in range(mine.shape[0])] + [(other, i) for i in range(other.shape[0])]

    def docs_of(ref, i):
        return jnp.broadcast_to(ref[i, tok : tok + 16, :tok].astype(F32)[0:1], (tok, tok))

    own_docs = docs_of(mine, 0).T
    ahead = lax.broadcasted_iota(jnp.int32, (tok, tok), 0) - lax.broadcasted_iota(
        jnp.int32, (tok, tok), 1
    )
    best = jnp.full((heads * tok, tok), -3e38, F32)
    for j, (ref, i) in enumerate(shards):
        score = lax.dot_general(
            stacked, ref[i, :tok, :HD], (((1,), (1,)), ((), ())), preferred_element_type=F32
        ) * (1.0 / math.sqrt(HD))
        allowed = (ahead >= start[j] - start[0]) & (own_docs == docs_of(ref, i))
        bias = jnp.where(allowed, 0.0, -1e30)
        score = score + jnp.concatenate([bias] * heads, 0)
        scores[:, j * tok : (j + 1) * tok] = score
        best = jnp.maximum(best, score)
    best = jnp.max(best, axis=1, keepdims=True)
    total = jnp.zeros((heads * tok, tok), F32)
    accum = jnp.zeros((heads * tok, HD), F32)
    for j, (ref, i) in enumerate(shards):
        expo = jnp.exp(scores[:, j * tok : (j + 1) * tok] - best)
        total = total + expo
        accum = accum + jnp.dot(
            expo.astype(BF16), ref[i, :tok, HD:], preferred_element_type=F32
        )
    result = (accum / jnp.sum(total, axis=1, keepdims=True)).astype(BF16)
    for i in range(heads):
        out[:, i * HD : (i + 1) * HD] = result[i * tok : (i + 1) * tok]


def attention(queries, mine, other, place):
    x_hi, y, core = place
    tok = queries.shape[0]
    start = []
    for c in (core, 1 - core):
        for xh in (x_hi, 1 - x_hi):
            for step in STEPS:
                start.append(((xh * NY + (y + step) % NY) * 2 + c) * tok)
    vmem = pl.BlockSpec(memory_space=pltpu.VMEM)
    return pl.pallas_call(
        attend,
        out_shape=jax.ShapeDtypeStruct(queries.shape, BF16),
        in_specs=[pl.BlockSpec(memory_space=pltpu.SMEM), vmem, vmem, vmem],
        out_specs=vmem,
        scratch_shapes=[pltpu.VMEM((queries.size // HD, 16 * tok), F32)],
        compiler_params=pltpu.CompilerParams(vmem_limit_bytes=24 * 2**20),
        cost_estimate=pl.CostEstimate(
            flops=4 * queries.size * 16 * tok, bytes_accessed=1600000, transcendentals=1600000
        ),
    )(jnp.stack(start).astype(jnp.int32), queries, mine, other)


def project(block, across, near, far, near_other, far_other, out):
    step, half = pl.program_id(0), pl.num_programs(0) // 2
    rows = out.shape[1] // 2
    both = jnp.concatenate(
        [block[...].reshape(NE, 1, rows, -1), across[...].reshape(NE, 1, rows, -1)], 1
    ).reshape(NE * 2 * rows, -1)

    def store(weight):
        product = jnp.dot(both, weight[...], preferred_element_type=F32)
        out[...] = product.astype(BF16).reshape(out.shape)

    pl.when(step < half - 1)(lambda: store(near))
    pl.when(step == half - 1)(lambda: store(far))
    pl.when((step >= half) & (step < 2 * half - 1))(lambda: store(near_other))
    pl.when(step == 2 * half - 1)(lambda: store(far_other))


def projection(block, across, near, far, near_other, far_other, rows):
    depth, part = far.shape
    whole = pl.BlockSpec(block.shape, lambda i: (0, 0))
    single = pl.BlockSpec((depth, part), lambda i: (0, 0))
    return pl.pallas_call(
        project,
        grid=(2 * NY,),
        out_shape=jax.ShapeDtypeStruct((NE, 2 * rows, 2 * NY * part), BF16),
        in_specs=[
            whole,
            whole,
            pl.BlockSpec((depth, part), lambda i: (0, jnp.minimum(i, NY - 2))),
            single,
            pl.BlockSpec((depth, part), lambda i: (0, jnp.clip(i - NY, 0, NY - 2))),
            single,
        ],
        out_specs=pl.BlockSpec((NE, 2 * rows, part), lambda i: (0, 0, i)),
        compiler_params=pltpu.CompilerParams(vmem_limit_bytes=24 * 2**20),
        cost_estimate=pl.CostEstimate(
            flops=16 * block.size * NY * part, bytes_accessed=6500000, transcendentals=0
        ),
    )(block, across, near, far, near_other, far_other)


def sum_and_sort(shift, terms, res_own, res_across, place, resid, outgoing):
    y, core = shift[0], shift[1]
    total = terms[0].astype(F32)
    for i in range(1, NE):
        total = total + terms[i].astype(F32)
    piece = total.shape[1] // (2 * NY)
    parts = [
        [total[:, (c * NY + i) * piece : (c * NY + i + 1) * piece] for i in (0, 1, 3, 2)]
        for c in range(2)
    ]
    for bit in (1, 2):
        moved = (y & bit) != 0
        parts = [
            [jnp.where(moved, row[(i - bit) % NY], row[i]) for i in range(NY)] for row in parts
        ]
    residual = jnp.concatenate([res_own[...], res_across[...]], 0).astype(F32)
    sums = []
    for i in range(NY):
        for c in range(2):
            value = jnp.where(core == 0, parts[c][i], parts[1 - c][i])
            columns = slice((2 * i + c) * piece, (2 * i + c + 1) * piece)
            sums.append((residual[:, columns] + value).astype(BF16))
    summed = jnp.concatenate(sums, 1)
    resid[...] = summed
    row = lax.broadcasted_iota(jnp.int32, (outgoing.shape[0], summed.shape[0]), 0)
    chosen = (row == place[0:1, :]) | (row == place[1:2, :])
    chosen = jnp.where(chosen, 1.0, 0.0).astype(BF16)
    outgoing[...] = jnp.dot(chosen, summed, preferred_element_type=F32).astype(BF16)


def residual_rows(y, core, terms, res_own, res_across, place):
    vmem = pl.BlockSpec(memory_space=pltpu.VMEM)
    rows, half = terms.shape[1:]
    return pl.pallas_call(
        sum_and_sort,
        out_shape=[
            jax.ShapeDtypeStruct((rows, half), BF16),
            jax.ShapeDtypeStruct((NE * 2 * CAP, half), BF16),
        ],
        in_specs=[pl.BlockSpec(memory_space=pltpu.SMEM)] + [vmem] * 4,
        out_specs=[vmem] * 2,
        compiler_params=pltpu.CompilerParams(vmem_limit_bytes=16 * 2**20),
        cost_estimate=pl.CostEstimate(
            flops=26000000, bytes_accessed=2600000, transcendentals=0
        ),
    )(jnp.stack([y, core]), terms, res_own, res_across, place)


def add_products(blocks, gain, weights, products, square):
    block = jnp.concatenate([b[...] for b in blocks], 0).astype(F32)
    scaled = (block * gain[...].astype(F32)).astype(BF16)
    squares = block * block
    lanes = square.shape[1]
    for i in range(squares.shape[1] // lanes):
        square[...] += squares[:, i * lanes : (i + 1) * lanes]
    for i, weight in enumerate(weights):
        products[i] += jnp.dot(scaled, weight[...], preferred_element_type=F32)


def begin(which, near, above, below, far, gain, g0, g1, u0, u1, products, square):
    @pl.when(pl.program_id(0) == 0)
    def _():
        products[...] = jnp.zeros_like(products)
        square[...] = jnp.zeros_like(square)

    add_products((near, above, below, far), gain, (g0, g1, u0, u1), products, square)


def finish(
    which, near, above, below, far, gain, before, squares, *refs
):
    weights, (own, other), (out, *firsts) = refs[:4], refs[4:6], refs[6:10]
    scaled, inner, outer, inner_sem, outer_sem = refs[10:]
    half = near.shape[1]
    width, unit = own.shape[1], own.shape[0]
    deep, wide = half // INNER, width // OUTER
    start = which[0] * half

    def inner_copy(i, part):
        rows = pl.ds(pl.multiple_of(start + part * deep, deep), deep)
        return pltpu.make_async_copy(
            weights[i].at[rows], inner.at[i, pl.ds(part * deep, deep)], inner_sem.at[i, part]
        )

    def outer_copy(i, part):
        columns = pl.ds(part * wide, wide)
        return pltpu.make_async_copy(
            (own, other)[i].at[:, columns], outer.at[i, :, columns], outer_sem.at[i, part]
        )

    for part in range(INNER):
        for i in range(4):
            inner_copy(i, part).start()
    for part in range(OUTER):
        for i in range(2):
            outer_copy(i, part).start()

    rows = near.shape[0]
    total = []
    for k, ref in enumerate((near, above, below, far)):
        block = ref[...].astype(F32)
        scaled[k * rows : (k + 1) * rows] = (block * gain[...].astype(F32)).astype(BF16)
        total.append(jnp.sum(block * block, axis=1, keepdims=True))
    square = jnp.concatenate(total, 0) + jnp.sum(squares[...], axis=1, keepdims=True)
    scale = lax.rsqrt(square / width + 1e-05)
    products = [before[i] for i in range(4)]
    for part in range(INNER):
        span = slice(part * deep, (part + 1) * deep)
        for i in range(4):
            inner_copy(i, part).wait()
            products[i] = products[i] + jnp.dot(
                scaled[:, span], inner[i, span], preferred_element_type=F32
            )
    first = which[1] == 0
    for i in range(2):
        gate = products[i] * scale
        hidden = gate / (1.0 + jnp.exp(-gate)) * (products[2 + i] * scale)
        hidden = hidden.reshape(NY, NE, 2, CAP, unit)
        even = hidden[:, :, 0].reshape(NY, NE * CAP, unit).astype(BF16)
        odd = hidden[:, :, 1].reshape(NY, NE * CAP, unit).astype(BF16)
        columns = slice(i * unit, (i + 1) * unit)
        out[0, :, :, columns] = jnp.where(first, even, odd)
        out[1, :, :, columns] = jnp.where(first, odd, even)
    sent = out[1, 1:].reshape(3 * NE * CAP, 2 * unit)
    for part in range(OUTER):
        columns = slice(part * wide, (part + 1) * wide)
        for i in range(2):
            outer_copy(i, part).wait()
        product = jnp.dot(sent[:, :unit], outer[0, :, columns], preferred_element_type=F32)
        product += jnp.dot(sent[:, unit:], outer[1, :, columns], preferred_element_type=F32)
        for k, ref in enumerate(firsts):
            ref[:, columns] = product[k * NE * CAP : (k + 1) * NE * CAP].astype(BF16)


def expert_rest(which, blocks, gain, before, weights, own, other):
    rows, half = blocks[0].shape
    unit, width = own.shape
    vmem, hbm = pl.BlockSpec(memory_space=pltpu.VMEM), pl.BlockSpec(memory_space=pl.ANY)
    return pl.pallas_call(
        finish,
        out_shape=[jax.ShapeDtypeStruct((2, NY, rows // 2, 2 * unit), BF16)]
        + [jax.ShapeDtypeStruct((rows // 2, width), BF16)] * 3,
        in_specs=[pl.BlockSpec(memory_space=pltpu.SMEM)] + [vmem] * (NY + 3) + [hbm] * 6,
        out_specs=[vmem] * 4,
        scratch_shapes=[
            pltpu.VMEM((NY * rows, half), BF16),
            pltpu.VMEM((4, half, unit), BF16),
            pltpu.VMEM((2, unit, width), BF16),
            pltpu.SemaphoreType.DMA((4, INNER)),
            pltpu.SemaphoreType.DMA((2, OUTER)),
        ],
        compiler_params=pltpu.CompilerParams(vmem_limit_bytes=42 * 2**20),
        cost_estimate=pl.CostEstimate(
            flops=12 * NY * rows * half * unit, bytes_accessed=26000000, transcendentals=600000
        ),
    )(which, *blocks, gain, *before, *weights, own, other)


def expert_in(which, blocks, gain, weights):
    rows, half = blocks[0].shape
    unit = weights[0].shape[1]
    part = 1024
    steps = half // part
    total = NY * rows
    sums = [(4, total, unit), (total, 128)]
    return pl.pallas_call(
        begin,
        grid_spec=pltpu.PrefetchScalarGridSpec(
            num_scalar_prefetch=1,
            grid=(steps,),
            in_specs=[pl.BlockSpec((rows, part), lambda k, w: (0, k))] * NY
            + [pl.BlockSpec((1, part), lambda k, w: (0, w[0] * steps + k))]
            + [pl.BlockSpec((part, unit), lambda k, w: (w[0] * steps + k, 0))] * 4,
            out_specs=[
                pl.BlockSpec(sums[0], lambda k, w: (0, 0, 0)),
                pl.BlockSpec(sums[1], lambda k, w: (0, 0)),
            ],
        ),
        out_shape=[jax.ShapeDtypeStruct(shape, F32) for shape in sums],
        compiler_params=pltpu.CompilerParams(vmem_limit_bytes=40 * 2**20),
        cost_estimate=pl.CostEstimate(
            flops=8 * total * half * unit, bytes_accessed=16000000, transcendentals=0
        ),
    )(which, *blocks, gain, *weights)


def down_rows(rows, split, hidden, own, other, *outs):
    units = own.shape[0]
    stacked = jnp.concatenate([hidden[a, k] for a, k in rows], 0)
    product = jnp.dot(stacked[:, :units], own[...], preferred_element_type=F32) + jnp.dot(
        stacked[:, units:], other[...], preferred_element_type=F32
    )
    product = product.astype(BF16)
    height = hidden.shape[2]
    step, steps = pl.program_id(0), pl.num_programs(0)
    at = 0
    for i in range(len(rows)):
        piece = product[i * height : (i + 1) * height]
        if i in split:
            for want, ref in ((step < steps // 2, outs[at]), (step >= steps // 2, outs[at + 1])):

                @pl.when(want)
                def _(ref=ref, piece=piece):
                    ref[...] = piece

            at += 2
        else:
            outs[at][...] = piece
            at += 1


def expert_out_part(hidden, own, other, rows, split=()):
    height, (units, width) = hidden.shape[2], own.shape
    part = 1024
    steps = width // part
    shapes, specs = [], []
    for i in range(len(rows)):
        if i in split:
            shapes += [jax.ShapeDtypeStruct((height, width // 2), BF16)] * 2
            specs += [
                pl.BlockSpec((height, part), lambda n: (0, jnp.minimum(n, steps // 2 - 1))),
                pl.BlockSpec((height, part), lambda n: (0, jnp.maximum(n - steps // 2, 0))),
            ]
        else:
            shapes.append(jax.ShapeDtypeStruct((height, width), BF16))
            specs.append(pl.BlockSpec((height, part), lambda n: (0, n)))
    return pl.pallas_call(
        functools.partial(down_rows, rows, split),
        grid=(steps,),
        out_shape=shapes,
        in_specs=[
            pl.BlockSpec(hidden.shape, lambda n: (0, 0, 0, 0)),
            pl.BlockSpec((units, part), lambda n: (0, n)),
            pl.BlockSpec((units, part), lambda n: (0, n)),
        ],
        out_specs=specs,
        compiler_params=pltpu.CompilerParams(vmem_limit_bytes=32 * 2**20),
        cost_estimate=pl.CostEstimate(
            flops=4 * len(rows) * height * units * width, bytes_accessed=15000000, transcendentals=0
        ),
    )(hidden, own, other)


def per_device(
    queries,
    k_load,
    v_load,
    kv_scale,
    doc_ids,
    residual_in,
    out_weight,
    norm_gain,
    w_gate,
    w_up,
    w_down,
    expert_ids,
    route_logit,
):
    ctx = lax.axis_index("ctx")
    x_hi, y, core = ctx // 8, (ctx // 2) % NY, ctx % 2
    tok = queries.shape[0]
    rows = residual_in.shape[0]
    width = residual_in.shape[1]
    half = width // 2
    gate_own, up_own, down_own = w_gate[0], w_up[0], w_down[0]

    ids = expert_ids.reshape(-1)
    key_value = packed_keys(k_load, v_load, kv_scale, doc_ids)
    out_weight, key_value = lax.optimization_barrier((out_weight, key_value))
    res_send = lax.dynamic_slice_in_dim(residual_in, (1 - x_hi) * half, half, 1)
    column = jnp.stack([key_value] + [from_y(key_value, step) for step in STEPS[1:]])
    near_pieces = [from_y(out_weight, 1), from_y(out_weight, -1)]
    mine = jnp.concatenate([column, flip_x(column)], 0)
    mine, *near_pieces = lax.optimization_barrier((mine, *near_pieces))
    other = flip_core(mine)
    cut = out_weight.shape[0] // 2
    far_halves = from_y(near_pieces[1][:cut], -1), from_y(near_pieces[0][cut:], 1)
    attn = attention(queries, mine, other, (x_hi, y, core))

    attn_across = flip_x(attn)
    near_mine = jnp.concatenate([out_weight, *near_pieces], 1)
    near_other = flip_core(near_mine)
    near_other, attn_across, far_lo, far_hi, res_send, early_ids = lax.optimization_barrier(
        (near_other, attn_across, *far_halves, res_send, ids)
    )
    far_mine = jnp.concatenate([far_lo, far_hi], 0)
    far_other = flip_core(far_mine)
    far_other, gate_own, up_own, down_own = lax.optimization_barrier(
        (far_other, gate_own, up_own, down_own)
    )
    res_across, across_ids = flip_x(res_send), flip_x(early_ids)
    partial = projection(
        attn, attn_across, near_mine, far_mine, near_other, far_other, rows
    )
    terms = lax.all_to_all(partial, "exp", split_axis=0, concat_axis=0, tiled=True)
    res_own = lax.dynamic_slice_in_dim(residual_in, x_hi * half, half, 1)

    slots_own = slots_of(ids)
    slots_across = slots_of(across_ids)
    place = jnp.concatenate(
        [
            (ids * 2 + x_hi) * CAP + slots_own,
            (across_ids * 2 + 1 - x_hi) * CAP + slots_across,
        ]
    ).reshape(2 * rows, TOP)
    resid, outgoing = residual_rows(y, core, terms, res_own, res_across, place.T)
    gate_other, up_other = flip_core(gate_own), flip_core(up_own)
    outgoing, gate_other, up_other = lax.optimization_barrier((outgoing, gate_other, up_other))
    arrived = lax.all_to_all(
        outgoing.reshape(NE, 2 * CAP, half), "exp", split_axis=0, concat_axis=0, tiled=True
    ).reshape(NE * 2 * CAP, half)
    down_other = flip_core(down_own)

    near, above, below, far = gather_y(arrived, 0)
    near_x = flip_x(near)
    above_x, below_x = from_y(near_x, 1), from_y(near_x, -1)
    far_x = flip_x(far)
    resid_across = flip_x(resid[rows:])
    gain = norm_gain.reshape(1, width)
    weights = (gate_own, gate_other, up_own, up_other)
    before = expert_in(x_hi[None], (near, above, below, far), gain, weights)
    *before, down_other = lax.optimization_barrier((*before, down_other))
    there = lax.dynamic_slice_in_dim(gain, (1 - x_hi) * half, half, 1)

    hidden, to_above, to_below, to_far = expert_rest(
        jnp.stack([1 - x_hi, x_hi]),
        (near_x, above_x, below_x, far_x),
        there,
        before,
        weights,
        down_own,
        down_other,
    )
    from_below = from_y(to_above, -1)
    from_above = from_y(to_below, 1)
    from_far = flip_x(to_far)
    above_lo, above_hi, below_lo, below_hi, cross, far_own, own = expert_out_part(
        hidden, down_own, down_other, ((0, 1), (0, 2), (1, 0), (0, 3), (0, 0)), (0, 1)
    )

    def added(*terms):
        return sum(t.astype(F32) for t in terms).astype(BF16)

    far_lo = from_y(added(far_own[:, :half], from_far[:, :half]), -1)
    far_hi = from_y(added(far_own[:, half:], from_far[:, half:]), 1)
    cross, above_hi, below_lo = lax.optimization_barrier(
        (added(cross, from_below, from_above), above_hi, below_lo)
    )
    from_cross = flip_x(cross)
    free_below = from_y(above_hi, -1)
    free_above = from_y(below_lo, 1)
    last_below = from_y(added(above_lo, far_lo), -1)
    last_above = from_y(added(below_hi, far_hi), 1)
    from_cross, last_below, last_above = lax.optimization_barrier(
        (from_cross, last_below, last_above)
    )
    expert_out = jnp.concatenate(
        [
            added(own[:, :half], from_cross[:, :half], free_above, last_below),
            added(own[:, half:], from_cross[:, half:], free_below, last_above),
        ],
        1,
    )

    returned = lax.all_to_all(
        expert_out.reshape(NE, CAP, width), "exp", split_axis=0, concat_axis=0, tiled=True
    ).reshape(NE * CAP, width)
    route = jax.nn.softmax(route_logit, axis=1)
    position = (ids * CAP + slots_own).reshape(rows, TOP)
    column = jnp.arange(NE * CAP, dtype=jnp.int32)[None, :]
    halves = [resid[:rows], resid_across]
    own_row = jnp.where(
        x_hi == 0, jnp.concatenate(halves, 1), jnp.concatenate(halves[::-1], 1)
    ).astype(F32)
    for k in range(TOP):
        chosen = (position[:, k : k + 1] == column).astype(BF16)
        own_row = own_row + route[:, k : k + 1] * jnp.dot(
            chosen, returned, preferred_element_type=F32
        )
    return own_row.astype(BF16)


def solution(mesh):
    return jax.shard_map(
        per_device,
        mesh=mesh,
        in_specs=(
            P("ctx", "exp"),
            P("ctx", "exp"),
            P("ctx", "exp"),
            P("ctx", "exp", None),
            P("ctx"),
            P(("ctx", "exp"), None),
            P("exp", "ctx"),
            P(),
            P("exp", None, "ctx"),
            P("exp", None, "ctx"),
            P("exp", "ctx", None),
            P(("ctx", "exp"), None),
            P(("ctx", "exp"), None),
        ),
        out_specs=P(("ctx", "exp"), None),
        check_vma=False,
    )
```

```python
import functools
import math

import jax
import jax.numpy as jnp
from jax import lax
from jax.experimental import pallas as pl
from jax.experimental.pallas import tpu as pltpu
from jax.sharding import PartitionSpec as P

HQ = 48
KVH = 8
HD = 128
KBLK = 16
TOP = 2
CAP = 8
NY = 4
NE = 8
BOTH = ("ctx", "exp")
F32 = jnp.float32
BF16 = jnp.bfloat16


def partner(flip_x=0, step_y=0, flip_core=0):
    pairs = []
    for source in range(128):
        ctx, exp = divmod(source, NE)
        x_hi, y, core = ctx // 8, (ctx // 2) % NY, ctx % 2
        target = ((x_hi ^ flip_x) * 8 + ((y + step_y) % NY) * 2 + (core ^ flip_core)) * NE + exp
        pairs.append((source, target))
    return pairs


def flip_x(value):
    return lax.ppermute(value, BOTH, partner(flip_x=1))


def flip_core(value):
    return lax.ppermute(value, BOTH, partner(flip_core=1))


def from_y(value, step):
    return lax.ppermute(value, BOTH, partner(step_y=-step))


def slots_of(ids):
    order = jnp.arange(ids.shape[0], dtype=jnp.int32)
    same = (ids[:, None] == ids[None, :]) & (order[None, :] < order[:, None])
    return jnp.sum(same.astype(jnp.int32), axis=1)


def gather_y(own, axis):
    half = own.shape[axis] // 2
    above = from_y(own, 1)
    below = from_y(own, -1)
    far_lo = from_y(lax.slice_in_dim(below, 0, half, axis=axis), -1)
    far_hi = from_y(lax.slice_in_dim(above, half, 2 * half, axis=axis), 1)
    far = lax.concatenate([far_lo, far_hi], axis)
    return own, above, below, far


STEPS = (0, 1, -1, 2)
INNER = 2
OUTER = 4


def pack(k_load, v_load, scales, docs, out, keys, values, sems):
    copies = [
        pltpu.make_async_copy(k_load, keys, sems.at[0]),
        pltpu.make_async_copy(v_load, values, sems.at[1]),
    ]
    for copy in copies:
        copy.start()
    tok = keys.shape[0]
    block = lax.broadcasted_iota(jnp.int32, (tok, tok // KBLK), 0) // KBLK
    group = lax.broadcasted_iota(jnp.int32, (tok, tok // KBLK), 1)
    picked = jnp.where(block == group, 1.0, 0.0).astype(BF16)
    factor = lax.dot_general(
        picked, scales[...], (((1,), (1,)), ((), ())), preferred_element_type=F32
    )
    wide = jnp.broadcast_to(docs[...].astype(F32), (16, tok)).astype(BF16)
    out[tok:, :HD] = wide
    out[tok:, HD:] = wide
    copies[0].wait()
    out[:tok, :HD] = (keys[...].astype(F32) * factor[:, 0:1]).astype(BF16)
    copies[1].wait()
    out[:tok, HD:] = (values[...].astype(F32) * factor[:, 1:2]).astype(BF16)


def packed_keys(k_load, v_load, kv_scale, doc_ids):
    vmem, hbm = pl.BlockSpec(memory_space=pltpu.VMEM), pl.BlockSpec(memory_space=pl.ANY)
    tok = k_load.shape[0]
    return pl.pallas_call(
        pack,
        out_shape=jax.ShapeDtypeStruct((tok + 16, 2 * HD), BF16),
        in_specs=[hbm, hbm, vmem, vmem],
        out_specs=vmem,
        scratch_shapes=[
            pltpu.VMEM(k_load.shape, BF16),
            pltpu.VMEM(v_load.shape, BF16),
            pltpu.SemaphoreType.DMA((2,)),
        ],
        compiler_params=pltpu.CompilerParams(vmem_limit_bytes=8 * 2**20),
        cost_estimate=pl.CostEstimate(flops=200000, bytes_accessed=200000, transcendentals=0),
    )(k_load, v_load, kv_scale[:, 0, :].T, doc_ids[None, :])


def attend(start, queries, mine, other, out, scores):
    tok = queries.shape[0]
    heads = queries.shape[1] // HD
    stacked = jnp.concatenate([queries[:, i * HD : (i + 1) * HD] for i in range(heads)], 0)
    shards = [(mine, i) for i in range(mine.shape[0])] + [(other, i) for i in range(other.shape[0])]

    def docs_of(ref, i):
        return jnp.broadcast_to(ref[i, tok : tok + 16, :tok].astype(F32)[0:1], (tok, tok))

    own_docs = docs_of(mine, 0).T
    ahead = lax.broadcasted_iota(jnp.int32, (tok, tok), 0) - lax.broadcasted_iota(
        jnp.int32, (tok, tok), 1
    )
    best = jnp.full((heads * tok, tok), -3e38, F32)
    for j, (ref, i) in enumerate(shards):
        score = lax.dot_general(
            stacked, ref[i, :tok, :HD], (((1,), (1,)), ((), ())), preferred_element_type=F32
        ) * (1.0 / math.sqrt(HD))
        allowed = (ahead >= start[j] - start[0]) & (own_docs == docs_of(ref, i))
        bias = jnp.where(allowed, 0.0, -1e30)
        score = score + jnp.concatenate([bias] * heads, 0)
        scores[:, j * tok : (j + 1) * tok] = score
        best = jnp.maximum(best, score)
    best = jnp.max(best, axis=1, keepdims=True)
    total = jnp.zeros((heads * tok, tok), F32)
    accum = jnp.zeros((heads * tok, HD), F32)
    for j, (ref, i) in enumerate(shards):
        expo = jnp.exp(scores[:, j * tok : (j + 1) * tok] - best)
        total = total + expo
        accum = accum + jnp.dot(
            expo.astype(BF16), ref[i, :tok, HD:], preferred_element_type=F32
        )
    result = (accum / jnp.sum(total, axis=1, keepdims=True)).astype(BF16)
    for i in range(heads):
        out[:, i * HD : (i + 1) * HD] = result[i * tok : (i + 1) * tok]


def attention(queries, mine, other, place):
    x_hi, y, core = place
    tok = queries.shape[0]
    start = []
    for c in (core, 1 - core):
        for xh in (x_hi, 1 - x_hi):
            for step in STEPS:
                start.append(((xh * NY + (y + step) % NY) * 2 + c) * tok)
    vmem = pl.BlockSpec(memory_space=pltpu.VMEM)
    return pl.pallas_call(
        attend,
        out_shape=jax.ShapeDtypeStruct(queries.shape, BF16),
        in_specs=[pl.BlockSpec(memory_space=pltpu.SMEM), vmem, vmem, vmem],
        out_specs=vmem,
        scratch_shapes=[pltpu.VMEM((queries.size // HD, 16 * tok), F32)],
        compiler_params=pltpu.CompilerParams(vmem_limit_bytes=40 * 2**20),
        cost_estimate=pl.CostEstimate(
            flops=4 * queries.size * 16 * tok, bytes_accessed=1600000, transcendentals=1600000
        ),
    )(jnp.stack(start).astype(jnp.int32), queries, mine, other)


def project(block, across, near, far, near_other, far_other, out):
    rows = out.shape[1] // 2
    both = jnp.concatenate(
        [block[...].reshape(NE, 1, rows, -1), across[...].reshape(NE, 1, rows, -1)], 1
    ).reshape(NE * 2 * rows, -1)
    part = far.shape[1]
    weights = [(ref, i) for ref in (near, far, near_other, far_other) for i in range(ref.shape[1] // part)]
    for n, (ref, i) in enumerate(weights):
        product = jnp.dot(both, ref[:, i * part : (i + 1) * part], preferred_element_type=F32)
        out[:, :, n * part : (n + 1) * part] = product.astype(BF16).reshape(NE, 2 * rows, part)


def projection(block, across, near, far, near_other, far_other, rows):
    vmem = pl.BlockSpec(memory_space=pltpu.VMEM)
    columns = 2 * (near.shape[1] + far.shape[1])
    return pl.pallas_call(
        project,
        out_shape=jax.ShapeDtypeStruct((NE, 2 * rows, columns), BF16),
        in_specs=[vmem] * 6,
        out_specs=vmem,
        compiler_params=pltpu.CompilerParams(vmem_limit_bytes=24 * 2**20),
        cost_estimate=pl.CostEstimate(
            flops=4 * block.size * columns, bytes_accessed=6500000, transcendentals=0
        ),
    )(block, across, near, far, near_other, far_other)


def sum_and_sort(shift, terms, res_own, res_across, place, resid, outgoing):
    y, core = shift[0], shift[1]
    total = terms[0].astype(F32)
    for i in range(1, NE):
        total = total + terms[i].astype(F32)
    piece = total.shape[1] // (2 * NY)
    parts = [
        [total[:, (c * NY + i) * piece : (c * NY + i + 1) * piece] for i in (0, 1, 3, 2)]
        for c in range(2)
    ]
    for bit in (1, 2):
        moved = (y & bit) != 0
        parts = [
            [jnp.where(moved, row[(i - bit) % NY], row[i]) for i in range(NY)] for row in parts
        ]
    residual = jnp.concatenate([res_own[...], res_across[...]], 0).astype(F32)
    sums = []
    for i in range(NY):
        for c in range(2):
            value = jnp.where(core == 0, parts[c][i], parts[1 - c][i])
            columns = slice((2 * i + c) * piece, (2 * i + c + 1) * piece)
            sums.append((residual[:, columns] + value).astype(BF16))
    summed = jnp.concatenate(sums, 1)
    resid[...] = summed
    row = lax.broadcasted_iota(jnp.int32, (outgoing.shape[0], summed.shape[0]), 0)
    chosen = (row == place[0:1, :]) | (row == place[1:2, :])
    chosen = jnp.where(chosen, 1.0, 0.0).astype(BF16)
    outgoing[...] = jnp.dot(chosen, summed, preferred_element_type=F32).astype(BF16)


def residual_rows(y, core, terms, res_own, res_across, place):
    vmem = pl.BlockSpec(memory_space=pltpu.VMEM)
    rows, half = terms.shape[1:]
    return pl.pallas_call(
        sum_and_sort,
        out_shape=[
            jax.ShapeDtypeStruct((rows, half), BF16),
            jax.ShapeDtypeStruct((NE * 2 * CAP, half), BF16),
        ],
        in_specs=[pl.BlockSpec(memory_space=pltpu.SMEM)] + [vmem] * 4,
        out_specs=[vmem] * 2,
        compiler_params=pltpu.CompilerParams(vmem_limit_bytes=16 * 2**20),
        cost_estimate=pl.CostEstimate(
            flops=26000000, bytes_accessed=2600000, transcendentals=0
        ),
    )(jnp.stack([y, core]), terms, res_own, res_across, place)


def add_products(blocks, gain, weights, products, square):
    block = jnp.concatenate([b[...] for b in blocks], 0).astype(F32)
    scaled = (block * gain[...].astype(F32)).astype(BF16)
    squares = block * block
    lanes = square.shape[1]
    for i in range(squares.shape[1] // lanes):
        square[...] += squares[:, i * lanes : (i + 1) * lanes]
    for i, weight in enumerate(weights):
        products[i] += jnp.dot(scaled, weight[...], preferred_element_type=F32)


def begin(which, near, above, below, far, gain, g0, g1, u0, u1, products, square):
    @pl.when(pl.program_id(0) == 0)
    def _():
        products[...] = jnp.zeros_like(products)
        square[...] = jnp.zeros_like(square)

    add_products((near, above, below, far), gain, (g0, g1, u0, u1), products, square)


def finish(
    which, near, above, below, far, gain, before, squares, *refs
):
    weights, (own, other), (out, *firsts) = refs[:4], refs[4:6], refs[6:10]
    scaled, inner, outer, inner_sem, outer_sem = refs[10:]
    half = near.shape[1]
    width, unit = own.shape[1], own.shape[0]
    deep, wide = half // INNER, width // OUTER
    start = which[0] * half

    def inner_copy(i, part):
        rows = pl.ds(pl.multiple_of(start + part * deep, deep), deep)
        return pltpu.make_async_copy(
            weights[i].at[rows], inner.at[i, pl.ds(part * deep, deep)], inner_sem.at[i, part]
        )

    def outer_copy(i, part):
        columns = pl.ds(part * wide, wide)
        return pltpu.make_async_copy(
            (own, other)[i].at[:, columns], outer.at[i, :, columns], outer_sem.at[i, part]
        )

    for part in range(INNER):
        for i in range(4):
            inner_copy(i, part).start()
    for part in range(OUTER):
        for i in range(2):
            outer_copy(i, part).start()

    rows = near.shape[0]
    total = []
    for k, ref in enumerate((near, above, below, far)):
        block = ref[...].astype(F32)
        scaled[k * rows : (k + 1) * rows] = (block * gain[...].astype(F32)).astype(BF16)
        total.append(jnp.sum(block * block, axis=1, keepdims=True))
    square = jnp.concatenate(total, 0) + jnp.sum(squares[...], axis=1, keepdims=True)
    scale = lax.rsqrt(square / width + 1e-05)
    products = [before[i] for i in range(4)]
    for part in range(INNER):
        span = slice(part * deep, (part + 1) * deep)
        for i in range(4):
            inner_copy(i, part).wait()
            products[i] = products[i] + jnp.dot(
                scaled[:, span], inner[i, span], preferred_element_type=F32
            )
    first = which[1] == 0
    for i in range(2):
        gate = products[i] * scale
        hidden = gate / (1.0 + jnp.exp(-gate)) * (products[2 + i] * scale)
        hidden = hidden.reshape(NY, NE, 2, CAP, unit)
        even = hidden[:, :, 0].reshape(NY, NE * CAP, unit).astype(BF16)
        odd = hidden[:, :, 1].reshape(NY, NE * CAP, unit).astype(BF16)
        columns = slice(i * unit, (i + 1) * unit)
        out[0, :, :, columns] = jnp.where(first, even, odd)
        out[1, :, :, columns] = jnp.where(first, odd, even)
    sent = out[1, 1:].reshape(3 * NE * CAP, 2 * unit)
    for part in range(OUTER):
        columns = slice(part * wide, (part + 1) * wide)
        for i in range(2):
            outer_copy(i, part).wait()
        product = jnp.dot(sent[:, :unit], outer[0, :, columns], preferred_element_type=F32)
        product += jnp.dot(sent[:, unit:], outer[1, :, columns], preferred_element_type=F32)
        for k, ref in enumerate(firsts):
            ref[:, columns] = product[k * NE * CAP : (k + 1) * NE * CAP].astype(BF16)


def expert_rest(which, blocks, gain, before, weights, own, other):
    rows, half = blocks[0].shape
    unit, width = own.shape
    vmem, hbm = pl.BlockSpec(memory_space=pltpu.VMEM), pl.BlockSpec(memory_space=pl.ANY)
    return pl.pallas_call(
        finish,
        out_shape=[jax.ShapeDtypeStruct((2, NY, rows // 2, 2 * unit), BF16)]
        + [jax.ShapeDtypeStruct((rows // 2, width), BF16)] * 3,
        in_specs=[pl.BlockSpec(memory_space=pltpu.SMEM)] + [vmem] * (NY + 3) + [hbm] * 6,
        out_specs=[vmem] * 4,
        scratch_shapes=[
            pltpu.VMEM((NY * rows, half), BF16),
            pltpu.VMEM((4, half, unit), BF16),
            pltpu.VMEM((2, unit, width), BF16),
            pltpu.SemaphoreType.DMA((4, INNER)),
            pltpu.SemaphoreType.DMA((2, OUTER)),
        ],
        compiler_params=pltpu.CompilerParams(vmem_limit_bytes=42 * 2**20),
        cost_estimate=pl.CostEstimate(
            flops=12 * NY * rows * half * unit, bytes_accessed=26000000, transcendentals=600000
        ),
    )(which, *blocks, gain, *before, *weights, own, other)


def expert_in(which, blocks, gain, weights):
    rows, half = blocks[0].shape
    unit = weights[0].shape[1]
    part = 1024
    steps = half // part
    total = NY * rows
    sums = [(4, total, unit), (total, 128)]
    return pl.pallas_call(
        begin,
        grid_spec=pltpu.PrefetchScalarGridSpec(
            num_scalar_prefetch=1,
            grid=(steps,),
            in_specs=[pl.BlockSpec((rows, part), lambda k, w: (0, k))] * NY
            + [pl.BlockSpec((1, part), lambda k, w: (0, w[0] * steps + k))]
            + [pl.BlockSpec((part, unit), lambda k, w: (w[0] * steps + k, 0))] * 4,
            out_specs=[
                pl.BlockSpec(sums[0], lambda k, w: (0, 0, 0)),
                pl.BlockSpec(sums[1], lambda k, w: (0, 0)),
            ],
        ),
        out_shape=[jax.ShapeDtypeStruct(shape, F32) for shape in sums],
        compiler_params=pltpu.CompilerParams(vmem_limit_bytes=40 * 2**20),
        cost_estimate=pl.CostEstimate(
            flops=8 * total * half * unit, bytes_accessed=16000000, transcendentals=0
        ),
    )(which, *blocks, gain, *weights)


def down_rows(rows, split, hidden, own, other, *outs):
    units = own.shape[0]
    stacked = jnp.concatenate([hidden[a, k] for a, k in rows], 0)
    product = jnp.dot(stacked[:, :units], own[...], preferred_element_type=F32) + jnp.dot(
        stacked[:, units:], other[...], preferred_element_type=F32
    )
    product = product.astype(BF16)
    height = hidden.shape[2]
    step, steps = pl.program_id(0), pl.num_programs(0)
    at = 0
    for i in range(len(rows)):
        piece = product[i * height : (i + 1) * height]
        if i in split:
            for want, ref in ((step < steps // 2, outs[at]), (step >= steps // 2, outs[at + 1])):

                @pl.when(want)
                def _(ref=ref, piece=piece):
                    ref[...] = piece

            at += 2
        else:
            outs[at][...] = piece
            at += 1


def expert_out_part(hidden, own, other, rows, split=()):
    height, (units, width) = hidden.shape[2], own.shape
    part = 1024
    steps = width // part
    shapes, specs = [], []
    for i in range(len(rows)):
        if i in split:
            shapes += [jax.ShapeDtypeStruct((height, width // 2), BF16)] * 2
            specs += [
                pl.BlockSpec((height, part), lambda n: (0, jnp.minimum(n, steps // 2 - 1))),
                pl.BlockSpec((height, part), lambda n: (0, jnp.maximum(n - steps // 2, 0))),
            ]
        else:
            shapes.append(jax.ShapeDtypeStruct((height, width), BF16))
            specs.append(pl.BlockSpec((height, part), lambda n: (0, n)))
    return pl.pallas_call(
        functools.partial(down_rows, rows, split),
        grid=(steps,),
        out_shape=shapes,
        in_specs=[
            pl.BlockSpec(hidden.shape, lambda n: (0, 0, 0, 0)),
            pl.BlockSpec((units, part), lambda n: (0, n)),
            pl.BlockSpec((units, part), lambda n: (0, n)),
        ],
        out_specs=specs,
        compiler_params=pltpu.CompilerParams(vmem_limit_bytes=32 * 2**20),
        cost_estimate=pl.CostEstimate(
            flops=4 * len(rows) * height * units * width, bytes_accessed=15000000, transcendentals=0
        ),
    )(hidden, own, other)


def per_device(
    queries,
    k_load,
    v_load,
    kv_scale,
    doc_ids,
    residual_in,
    out_weight,
    norm_gain,
    w_gate,
    w_up,
    w_down,
    expert_ids,
    route_logit,
):
    ctx = lax.axis_index("ctx")
    x_hi, y, core = ctx // 8, (ctx // 2) % NY, ctx % 2
    tok = queries.shape[0]
    rows = residual_in.shape[0]
    width = residual_in.shape[1]
    half = width // 2
    gate_own, up_own, down_own = w_gate[0], w_up[0], w_down[0]

    ids = expert_ids.reshape(-1)
    key_value = packed_keys(k_load, v_load, kv_scale, doc_ids)
    out_weight, key_value = lax.optimization_barrier((out_weight, key_value))
    res_send = lax.dynamic_slice_in_dim(residual_in, (1 - x_hi) * half, half, 1)
    column = jnp.stack([key_value] + [from_y(key_value, step) for step in STEPS[1:]])
    near_pieces = [from_y(out_weight, 1), from_y(out_weight, -1)]
    mine = jnp.concatenate([column, flip_x(column)], 0)
    mine, *near_pieces = lax.optimization_barrier((mine, *near_pieces))
    other = flip_core(mine)
    cut = out_weight.shape[0] // 2
    far_halves = from_y(near_pieces[1][:cut], -1), from_y(near_pieces[0][cut:], 1)
    attn = attention(queries, mine, other, (x_hi, y, core))

    attn_across = flip_x(attn)
    near_mine = jnp.concatenate([out_weight, *near_pieces], 1)
    near_other = flip_core(near_mine)
    near_other, attn_across, far_lo, far_hi, res_send, early_ids = lax.optimization_barrier(
        (near_other, attn_across, *far_halves, res_send, ids)
    )
    far_mine = jnp.concatenate([far_lo, far_hi], 0)
    far_other = flip_core(far_mine)
    far_other, gate_own, up_own, down_own = lax.optimization_barrier(
        (far_other, gate_own, up_own, down_own)
    )
    res_across, across_ids = flip_x(res_send), flip_x(early_ids)
    partial = projection(
        attn, attn_across, near_mine, far_mine, near_other, far_other, rows
    )
    terms = lax.all_to_all(partial, "exp", split_axis=0, concat_axis=0, tiled=True)
    res_own = lax.dynamic_slice_in_dim(residual_in, x_hi * half, half, 1)

    slots_own = slots_of(ids)
    slots_across = slots_of(across_ids)
    place = jnp.concatenate(
        [
            (ids * 2 + x_hi) * CAP + slots_own,
            (across_ids * 2 + 1 - x_hi) * CAP + slots_across,
        ]
    ).reshape(2 * rows, TOP)
    resid, outgoing = residual_rows(y, core, terms, res_own, res_across, place.T)
    gate_other, up_other = flip_core(gate_own), flip_core(up_own)
    outgoing, gate_other, up_other = lax.optimization_barrier((outgoing, gate_other, up_other))
    arrived = lax.all_to_all(
        outgoing.reshape(NE, 2 * CAP, half), "exp", split_axis=0, concat_axis=0, tiled=True
    ).reshape(NE * 2 * CAP, half)
    down_other = flip_core(down_own)

    near, above, below, far = gather_y(arrived, 0)
    near_x = flip_x(near)
    above_x, below_x = from_y(near_x, 1), from_y(near_x, -1)
    far_x = flip_x(far)
    resid_across = flip_x(resid[rows:])
    gain = norm_gain.reshape(1, width)
    weights = (gate_own, gate_other, up_own, up_other)
    before = expert_in(x_hi[None], (near, above, below, far), gain, weights)
    *before, down_other = lax.optimization_barrier((*before, down_other))
    there = lax.dynamic_slice_in_dim(gain, (1 - x_hi) * half, half, 1)

    hidden, to_above, to_below, to_far = expert_rest(
        jnp.stack([1 - x_hi, x_hi]),
        (near_x, above_x, below_x, far_x),
        there,
        before,
        weights,
        down_own,
        down_other,
    )
    from_below = from_y(to_above, -1)
    from_above = from_y(to_below, 1)
    from_far = flip_x(to_far)
    above_lo, above_hi, below_lo, below_hi, cross, far_own, own = expert_out_part(
        hidden, down_own, down_other, ((0, 1), (0, 2), (1, 0), (0, 3), (0, 0)), (0, 1)
    )

    def added(*terms):
        return sum(t.astype(F32) for t in terms).astype(BF16)

    far_lo = from_y(added(far_own[:, :half], from_far[:, :half]), -1)
    far_hi = from_y(added(far_own[:, half:], from_far[:, half:]), 1)
    cross, above_hi, below_lo = lax.optimization_barrier(
        (added(cross, from_below, from_above), above_hi, below_lo)
    )
    from_cross = flip_x(cross)
    free_below = from_y(above_hi, -1)
    free_above = from_y(below_lo, 1)
    last_below = from_y(added(above_lo, far_lo), -1)
    last_above = from_y(added(below_hi, far_hi), 1)
    from_cross, last_below, last_above = lax.optimization_barrier(
        (from_cross, last_below, last_above)
    )
    expert_out = jnp.concatenate(
        [
            added(own[:, :half], from_cross[:, :half], free_above, last_below),
            added(own[:, half:], from_cross[:, half:], free_below, last_above),
        ],
        1,
    )

    returned = lax.all_to_all(
        expert_out.reshape(NE, CAP, width), "exp", split_axis=0, concat_axis=0, tiled=True
    ).reshape(NE * CAP, width)
    route = jax.nn.softmax(route_logit, axis=1)
    position = (ids * CAP + slots_own).reshape(rows, TOP)
    column = jnp.arange(NE * CAP, dtype=jnp.int32)[None, :]
    halves = [resid[:rows], resid_across]
    own_row = jnp.where(
        x_hi == 0, jnp.concatenate(halves, 1), jnp.concatenate(halves[::-1], 1)
    ).astype(F32)
    for k in range(TOP):
        chosen = (position[:, k : k + 1] == column).astype(BF16)
        own_row = own_row + route[:, k : k + 1] * jnp.dot(
            chosen, returned, preferred_element_type=F32
        )
    return own_row.astype(BF16)


def solution(mesh):
    return jax.shard_map(
        per_device,
        mesh=mesh,
        in_specs=(
            P("ctx", "exp"),
            P("ctx", "exp"),
            P("ctx", "exp"),
            P("ctx", "exp", None),
            P("ctx"),
            P(("ctx", "exp"), None),
            P("exp", "ctx"),
            P(),
            P("exp", None, "ctx"),
            P("exp", None, "ctx"),
            P("exp", "ctx", None),
            P(("ctx", "exp"), None),
            P(("ctx", "exp"), None),
        ),
        out_specs=P(("ctx", "exp"), None),
        check_vma=False,
    )
```

```python
import functools
import math

import jax
import jax.numpy as jnp
from jax import lax
from jax.experimental import pallas as pl
from jax.experimental.pallas import tpu as pltpu
from jax.sharding import PartitionSpec as P

HQ = 48
KVH = 8
HD = 128
KBLK = 16
TOP = 2
CAP = 8
NY = 4
NE = 8
BOTH = ("ctx", "exp")
F32 = jnp.float32
BF16 = jnp.bfloat16


def partner(flip_x=0, step_y=0, flip_core=0):
    pairs = []
    for source in range(128):
        ctx, exp = divmod(source, NE)
        x_hi, y, core = ctx // 8, (ctx // 2) % NY, ctx % 2
        target = ((x_hi ^ flip_x) * 8 + ((y + step_y) % NY) * 2 + (core ^ flip_core)) * NE + exp
        pairs.append((source, target))
    return pairs


def flip_x(value):
    return lax.ppermute(value, BOTH, partner(flip_x=1))


def flip_core(value):
    return lax.ppermute(value, BOTH, partner(flip_core=1))


def from_y(value, step):
    return lax.ppermute(value, BOTH, partner(step_y=-step))


def slots_of(ids):
    order = jnp.arange(ids.shape[0], dtype=jnp.int32)
    same = (ids[:, None] == ids[None, :]) & (order[None, :] < order[:, None])
    return jnp.sum(same.astype(jnp.int32), axis=1)


def gather_y(own, axis):
    half = own.shape[axis] // 2
    above = from_y(own, 1)
    below = from_y(own, -1)
    far_lo = from_y(lax.slice_in_dim(below, 0, half, axis=axis), -1)
    far_hi = from_y(lax.slice_in_dim(above, half, 2 * half, axis=axis), 1)
    far = lax.concatenate([far_lo, far_hi], axis)
    return own, above, below, far


STEPS = (0, 1, -1, 2)
INNER = 2
OUTER = 2


def pack(k_load, v_load, scales, docs, out, keys, values, sems):
    copies = [
        pltpu.make_async_copy(k_load, keys, sems.at[0]),
        pltpu.make_async_copy(v_load, values, sems.at[1]),
    ]
    for copy in copies:
        copy.start()
    tok = keys.shape[0]
    block = lax.broadcasted_iota(jnp.int32, (tok, tok // KBLK), 0) // KBLK
    group = lax.broadcasted_iota(jnp.int32, (tok, tok // KBLK), 1)
    picked = jnp.where(block == group, 1.0, 0.0).astype(BF16)
    factor = lax.dot_general(
        picked, scales[...], (((1,), (1,)), ((), ())), preferred_element_type=F32
    )
    wide = jnp.broadcast_to(docs[...].astype(F32), (16, tok)).astype(BF16)
    out[tok:, :HD] = wide
    out[tok:, HD:] = wide
    copies[0].wait()
    out[:tok, :HD] = (keys[...].astype(F32) * factor[:, 0:1]).astype(BF16)
    copies[1].wait()
    out[:tok, HD:] = (values[...].astype(F32) * factor[:, 1:2]).astype(BF16)


def packed_keys(k_load, v_load, kv_scale, doc_ids):
    vmem, hbm = pl.BlockSpec(memory_space=pltpu.VMEM), pl.BlockSpec(memory_space=pl.ANY)
    tok = k_load.shape[0]
    return pl.pallas_call(
        pack,
        out_shape=jax.ShapeDtypeStruct((tok + 16, 2 * HD), BF16),
        in_specs=[hbm, hbm, vmem, vmem],
        out_specs=vmem,
        scratch_shapes=[
            pltpu.VMEM(k_load.shape, BF16),
            pltpu.VMEM(v_load.shape, BF16),
            pltpu.SemaphoreType.DMA((2,)),
        ],
        compiler_params=pltpu.CompilerParams(vmem_limit_bytes=8 * 2**20),
        cost_estimate=pl.CostEstimate(flops=200000, bytes_accessed=200000, transcendentals=0),
    )(k_load, v_load, kv_scale[:, 0, :].T, doc_ids[None, :])


def attend(start, queries, mine, other, out, scores):
    tok = queries.shape[0]
    heads = queries.shape[1] // HD
    stacked = jnp.concatenate([queries[:, i * HD : (i + 1) * HD] for i in range(heads)], 0)
    shards = [(mine, i) for i in range(mine.shape[0])] + [(other, i) for i in range(other.shape[0])]

    def docs_of(ref, i):
        return jnp.broadcast_to(ref[i, tok : tok + 16, :tok].astype(F32)[0:1], (tok, tok))

    own_docs = docs_of(mine, 0).T
    ahead = lax.broadcasted_iota(jnp.int32, (tok, tok), 0) - lax.broadcasted_iota(
        jnp.int32, (tok, tok), 1
    )
    best = jnp.full((heads * tok, tok), -3e38, F32)
    for j, (ref, i) in enumerate(shards):
        score = lax.dot_general(
            stacked, ref[i, :tok, :HD], (((1,), (1,)), ((), ())), preferred_element_type=F32
        ) * (1.0 / math.sqrt(HD))
        allowed = (ahead >= start[j] - start[0]) & (own_docs == docs_of(ref, i))
        bias = jnp.where(allowed, 0.0, -1e30)
        score = score + jnp.concatenate([bias] * heads, 0)
        scores[:, j * tok : (j + 1) * tok] = score
        best = jnp.maximum(best, score)
    best = jnp.max(best, axis=1, keepdims=True)
    total = jnp.zeros((heads * tok, tok), F32)
    accum = jnp.zeros((heads * tok, HD), F32)
    for j, (ref, i) in enumerate(shards):
        expo = jnp.exp(scores[:, j * tok : (j + 1) * tok] - best)
        total = total + expo
        accum = accum + jnp.dot(
            expo.astype(BF16), ref[i, :tok, HD:], preferred_element_type=F32
        )
    result = (accum / jnp.sum(total, axis=1, keepdims=True)).astype(BF16)
    for i in range(heads):
        out[:, i * HD : (i + 1) * HD] = result[i * tok : (i + 1) * tok]


def attention(queries, mine, other, place):
    x_hi, y, core = place
    tok = queries.shape[0]
    start = []
    for c in (core, 1 - core):
        for xh in (x_hi, 1 - x_hi):
            for step in STEPS:
                start.append(((xh * NY + (y + step) % NY) * 2 + c) * tok)
    vmem = pl.BlockSpec(memory_space=pltpu.VMEM)
    return pl.pallas_call(
        attend,
        out_shape=jax.ShapeDtypeStruct(queries.shape, BF16),
        in_specs=[pl.BlockSpec(memory_space=pltpu.SMEM), vmem, vmem, vmem],
        out_specs=vmem,
        scratch_shapes=[pltpu.VMEM((queries.size // HD, 16 * tok), F32)],
        compiler_params=pltpu.CompilerParams(vmem_limit_bytes=40 * 2**20),
        cost_estimate=pl.CostEstimate(
            flops=4 * queries.size * 16 * tok, bytes_accessed=1600000, transcendentals=1600000
        ),
    )(jnp.stack(start).astype(jnp.int32), queries, mine, other)


def project(block, across, near, far, near_other, far_other, out):
    rows = out.shape[1] // 2
    both = jnp.concatenate(
        [block[...].reshape(NE, 1, rows, -1), across[...].reshape(NE, 1, rows, -1)], 1
    ).reshape(NE * 2 * rows, -1)
    part = far.shape[1]
    weights = [(ref, i) for ref in (near, far, near_other, far_other) for i in range(ref.shape[1] // part)]
    for n, (ref, i) in enumerate(weights):
        product = jnp.dot(both, ref[:, i * part : (i + 1) * part], preferred_element_type=F32)
        out[:, :, n * part : (n + 1) * part] = product.astype(BF16).reshape(NE, 2 * rows, part)


def projection(block, across, near, far, near_other, far_other, rows):
    vmem = pl.BlockSpec(memory_space=pltpu.VMEM)
    columns = 2 * (near.shape[1] + far.shape[1])
    return pl.pallas_call(
        project,
        out_shape=jax.ShapeDtypeStruct((NE, 2 * rows, columns), BF16),
        in_specs=[vmem] * 6,
        out_specs=vmem,
        compiler_params=pltpu.CompilerParams(vmem_limit_bytes=24 * 2**20),
        cost_estimate=pl.CostEstimate(
            flops=4 * block.size * columns, bytes_accessed=6500000, transcendentals=0
        ),
    )(block, across, near, far, near_other, far_other)


def sum_and_sort(shift, terms, res_own, res_across, place, resid, outgoing):
    y, core = shift[0], shift[1]
    total = terms[0].astype(F32)
    for i in range(1, NE):
        total = total + terms[i].astype(F32)
    piece = total.shape[1] // (2 * NY)
    parts = [
        [total[:, (c * NY + i) * piece : (c * NY + i + 1) * piece] for i in (0, 1, 3, 2)]
        for c in range(2)
    ]
    for bit in (1, 2):
        moved = (y & bit) != 0
        parts = [
            [jnp.where(moved, row[(i - bit) % NY], row[i]) for i in range(NY)] for row in parts
        ]
    residual = jnp.concatenate([res_own[...], res_across[...]], 0).astype(F32)
    sums = []
    for i in range(NY):
        for c in range(2):
            value = jnp.where(core == 0, parts[c][i], parts[1 - c][i])
            columns = slice((2 * i + c) * piece, (2 * i + c + 1) * piece)
            sums.append((residual[:, columns] + value).astype(BF16))
    summed = jnp.concatenate(sums, 1)
    resid[...] = summed
    row = lax.broadcasted_iota(jnp.int32, (outgoing.shape[0], summed.shape[0]), 0)
    chosen = (row == place[0:1, :]) | (row == place[1:2, :])
    chosen = jnp.where(chosen, 1.0, 0.0).astype(BF16)
    outgoing[...] = jnp.dot(chosen, summed, preferred_element_type=F32).astype(BF16)


def residual_rows(y, core, terms, res_own, res_across, place):
    vmem = pl.BlockSpec(memory_space=pltpu.VMEM)
    rows, half = terms.shape[1:]
    return pl.pallas_call(
        sum_and_sort,
        out_shape=[
            jax.ShapeDtypeStruct((rows, half), BF16),
            jax.ShapeDtypeStruct((NE * 2 * CAP, half), BF16),
        ],
        in_specs=[pl.BlockSpec(memory_space=pltpu.SMEM)] + [vmem] * 4,
        out_specs=[vmem] * 2,
        compiler_params=pltpu.CompilerParams(vmem_limit_bytes=16 * 2**20),
        cost_estimate=pl.CostEstimate(
            flops=26000000, bytes_accessed=2600000, transcendentals=0
        ),
    )(jnp.stack([y, core]), terms, res_own, res_across, place)


def add_products(blocks, gain, weights, products, square):
    block = jnp.concatenate([b[...] for b in blocks], 0).astype(F32)
    scaled = (block * gain[...].astype(F32)).astype(BF16)
    squares = block * block
    lanes = square.shape[1]
    for i in range(squares.shape[1] // lanes):
        square[...] += squares[:, i * lanes : (i + 1) * lanes]
    for i, weight in enumerate(weights):
        products[i] += jnp.dot(scaled, weight[...], preferred_element_type=F32)


def begin(which, near, above, below, far, gain, g0, g1, u0, u1, products, square):
    @pl.when(pl.program_id(0) == 0)
    def _():
        products[...] = jnp.zeros_like(products)
        square[...] = jnp.zeros_like(square)

    add_products((near, above, below, far), gain, (g0, g1, u0, u1), products, square)


def finish(
    which, near, above, below, far, gain, before, squares, *refs
):
    weights, (own, other), (out, *firsts) = refs[:4], refs[4:6], refs[6:10]
    scaled, inner, outer, inner_sem, outer_sem = refs[10:]
    half = near.shape[1]
    width, unit = own.shape[1], own.shape[0]
    deep, wide = half // INNER, width // OUTER
    start = which[0] * half

    def inner_copy(i, part):
        rows = pl.ds(pl.multiple_of(start + part * deep, deep), deep)
        return pltpu.make_async_copy(
            weights[i].at[rows], inner.at[i, pl.ds(part * deep, deep)], inner_sem.at[i, part]
        )

    def outer_copy(i, part):
        columns = pl.ds(part * wide, wide)
        return pltpu.make_async_copy(
            (own, other)[i].at[:, columns], outer.at[i, :, columns], outer_sem.at[i, part]
        )

    for part in range(INNER):
        for i in range(4):
            inner_copy(i, part).start()
    for part in range(OUTER):
        for i in range(2):
            outer_copy(i, part).start()

    rows = near.shape[0]
    total = []
    for k, ref in enumerate((near, above, below, far)):
        block = ref[...].astype(F32)
        scaled[k * rows : (k + 1) * rows] = (block * gain[...].astype(F32)).astype(BF16)
        total.append(jnp.sum(block * block, axis=1, keepdims=True))
    square = jnp.concatenate(total, 0) + jnp.sum(squares[...], axis=1, keepdims=True)
    scale = lax.rsqrt(square / width + 1e-05)
    products = [before[i] for i in range(4)]
    for part in range(INNER):
        span = slice(part * deep, (part + 1) * deep)
        for i in range(4):
            inner_copy(i, part).wait()
            products[i] = products[i] + jnp.dot(
                scaled[:, span], inner[i, span], preferred_element_type=F32
            )
    first = which[1] == 0
    for i in range(2):
        gate = products[i] * scale
        hidden = gate / (1.0 + jnp.exp(-gate)) * (products[2 + i] * scale)
        hidden = hidden.reshape(NY, NE, 2, CAP, unit)
        even = hidden[:, :, 0].reshape(NY, NE * CAP, unit).astype(BF16)
        odd = hidden[:, :, 1].reshape(NY, NE * CAP, unit).astype(BF16)
        columns = slice(i * unit, (i + 1) * unit)
        out[0, :, :, columns] = jnp.where(first, even, odd)
        out[1, :, :, columns] = jnp.where(first, odd, even)
    sent = out[1, 1:].reshape(3 * NE * CAP, 2 * unit)
    for part in range(OUTER):
        columns = slice(part * wide, (part + 1) * wide)
        for i in range(2):
            outer_copy(i, part).wait()
        product = jnp.dot(sent[:, :unit], outer[0, :, columns], preferred_element_type=F32)
        product += jnp.dot(sent[:, unit:], outer[1, :, columns], preferred_element_type=F32)
        for k, ref in enumerate(firsts):
            ref[:, columns] = product[k * NE * CAP : (k + 1) * NE * CAP].astype(BF16)


def expert_rest(which, blocks, gain, before, weights, own, other):
    rows, half = blocks[0].shape
    unit, width = own.shape
    vmem, hbm = pl.BlockSpec(memory_space=pltpu.VMEM), pl.BlockSpec(memory_space=pl.ANY)
    return pl.pallas_call(
        finish,
        out_shape=[jax.ShapeDtypeStruct((2, NY, rows // 2, 2 * unit), BF16)]
        + [jax.ShapeDtypeStruct((rows // 2, width), BF16)] * 3,
        in_specs=[pl.BlockSpec(memory_space=pltpu.SMEM)] + [vmem] * (NY + 3) + [hbm] * 6,
        out_specs=[vmem] * 4,
        scratch_shapes=[
            pltpu.VMEM((NY * rows, half), BF16),
            pltpu.VMEM((4, half, unit), BF16),
            pltpu.VMEM((2, unit, width), BF16),
            pltpu.SemaphoreType.DMA((4, INNER)),
            pltpu.SemaphoreType.DMA((2, OUTER)),
        ],
        compiler_params=pltpu.CompilerParams(vmem_limit_bytes=42 * 2**20),
        cost_estimate=pl.CostEstimate(
            flops=12 * NY * rows * half * unit, bytes_accessed=26000000, transcendentals=600000
        ),
    )(which, *blocks, gain, *before, *weights, own, other)


def expert_in(which, blocks, gain, weights):
    rows, half = blocks[0].shape
    unit = weights[0].shape[1]
    part = 1024
    steps = half // part
    total = NY * rows
    sums = [(4, total, unit), (total, 128)]
    return pl.pallas_call(
        begin,
        grid_spec=pltpu.PrefetchScalarGridSpec(
            num_scalar_prefetch=1,
            grid=(steps,),
            in_specs=[pl.BlockSpec((rows, part), lambda k, w: (0, k))] * NY
            + [pl.BlockSpec((1, part), lambda k, w: (0, w[0] * steps + k))]
            + [pl.BlockSpec((part, unit), lambda k, w: (w[0] * steps + k, 0))] * 4,
            out_specs=[
                pl.BlockSpec(sums[0], lambda k, w: (0, 0, 0)),
                pl.BlockSpec(sums[1], lambda k, w: (0, 0)),
            ],
        ),
        out_shape=[jax.ShapeDtypeStruct(shape, F32) for shape in sums],
        compiler_params=pltpu.CompilerParams(vmem_limit_bytes=40 * 2**20),
        cost_estimate=pl.CostEstimate(
            flops=8 * total * half * unit, bytes_accessed=16000000, transcendentals=0
        ),
    )(which, *blocks, gain, *weights)


def down_rows(rows, split, hidden, own, other, *outs):
    units = own.shape[0]
    stacked = jnp.concatenate([hidden[a, k] for a, k in rows], 0)
    product = jnp.dot(stacked[:, :units], own[...], preferred_element_type=F32) + jnp.dot(
        stacked[:, units:], other[...], preferred_element_type=F32
    )
    product = product.astype(BF16)
    height = hidden.shape[2]
    step, steps = pl.program_id(0), pl.num_programs(0)
    at = 0
    for i in range(len(rows)):
        piece = product[i * height : (i + 1) * height]
        if i in split:
            for want, ref in ((step < steps // 2, outs[at]), (step >= steps // 2, outs[at + 1])):

                @pl.when(want)
                def _(ref=ref, piece=piece):
                    ref[...] = piece

            at += 2
        else:
            outs[at][...] = piece
            at += 1


def expert_out_part(hidden, own, other, rows, split=()):
    height, (units, width) = hidden.shape[2], own.shape
    part = 1024
    steps = width // part
    shapes, specs = [], []
    for i in range(len(rows)):
        if i in split:
            shapes += [jax.ShapeDtypeStruct((height, width // 2), BF16)] * 2
            specs += [
                pl.BlockSpec((height, part), lambda n: (0, jnp.minimum(n, steps // 2 - 1))),
                pl.BlockSpec((height, part), lambda n: (0, jnp.maximum(n - steps // 2, 0))),
            ]
        else:
            shapes.append(jax.ShapeDtypeStruct((height, width), BF16))
            specs.append(pl.BlockSpec((height, part), lambda n: (0, n)))
    return pl.pallas_call(
        functools.partial(down_rows, rows, split),
        grid=(steps,),
        out_shape=shapes,
        in_specs=[
            pl.BlockSpec(hidden.shape, lambda n: (0, 0, 0, 0)),
            pl.BlockSpec((units, part), lambda n: (0, n)),
            pl.BlockSpec((units, part), lambda n: (0, n)),
        ],
        out_specs=specs,
        compiler_params=pltpu.CompilerParams(vmem_limit_bytes=32 * 2**20),
        cost_estimate=pl.CostEstimate(
            flops=4 * len(rows) * height * units * width, bytes_accessed=15000000, transcendentals=0
        ),
    )(hidden, own, other)


def settle(own, cross, free_above, last_below, free_below, last_above, out):
    half = free_above.shape[1]
    for columns, free, last in (
        (slice(0, half), free_above, last_below),
        (slice(half, 2 * half), free_below, last_above),
    ):
        total = own[:, columns].astype(F32) + cross[:, columns].astype(F32)
        total = total + free[...].astype(F32) + last[...].astype(F32)
        out[:, columns] = total.astype(BF16)


def last_sum(*terms):
    vmem = pl.BlockSpec(memory_space=pltpu.VMEM)
    return pl.pallas_call(
        settle,
        out_shape=jax.ShapeDtypeStruct(terms[0].shape, BF16),
        in_specs=[vmem] * len(terms),
        out_specs=vmem,
        compiler_params=pltpu.CompilerParams(vmem_limit_bytes=16 * 2**20),
        cost_estimate=pl.CostEstimate(
            flops=4 * terms[0].size, bytes_accessed=10 * terms[0].size, transcendentals=0
        ),
    )(*terms)


def per_device(
    queries,
    k_load,
    v_load,
    kv_scale,
    doc_ids,
    residual_in,
    out_weight,
    norm_gain,
    w_gate,
    w_up,
    w_down,
    expert_ids,
    route_logit,
):
    ctx = lax.axis_index("ctx")
    x_hi, y, core = ctx // 8, (ctx // 2) % NY, ctx % 2
    tok = queries.shape[0]
    rows = residual_in.shape[0]
    width = residual_in.shape[1]
    half = width // 2
    gate_own, up_own, down_own = w_gate[0], w_up[0], w_down[0]

    ids = expert_ids.reshape(-1)
    key_value = packed_keys(k_load, v_load, kv_scale, doc_ids)
    out_weight, key_value = lax.optimization_barrier((out_weight, key_value))
    res_send = lax.dynamic_slice_in_dim(residual_in, (1 - x_hi) * half, half, 1)
    column = jnp.stack([key_value] + [from_y(key_value, step) for step in STEPS[1:]])
    near_pieces = [from_y(out_weight, 1), from_y(out_weight, -1)]
    mine = jnp.concatenate([column, flip_x(column)], 0)
    mine, *near_pieces = lax.optimization_barrier((mine, *near_pieces))
    other = flip_core(mine)
    cut = out_weight.shape[0] // 2
    far_halves = from_y(near_pieces[1][:cut], -1), from_y(near_pieces[0][cut:], 1)
    attn = attention(queries, mine, other, (x_hi, y, core))

    attn_across = flip_x(attn)
    near_mine = jnp.concatenate([out_weight, *near_pieces], 1)
    near_other = flip_core(near_mine)
    near_other, attn_across, far_lo, far_hi, res_send, early_ids = lax.optimization_barrier(
        (near_other, attn_across, *far_halves, res_send, ids)
    )
    far_mine = jnp.concatenate([far_lo, far_hi], 0)
    far_other = flip_core(far_mine)
    far_other, gate_own, up_own, down_own = lax.optimization_barrier(
        (far_other, gate_own, up_own, down_own)
    )
    res_across, across_ids = flip_x(res_send), flip_x(early_ids)
    partial = projection(
        attn, attn_across, near_mine, far_mine, near_other, far_other, rows
    )
    terms = lax.all_to_all(partial, "exp", split_axis=0, concat_axis=0, tiled=True)
    res_own = lax.dynamic_slice_in_dim(residual_in, x_hi * half, half, 1)

    slots_own = slots_of(ids)
    slots_across = slots_of(across_ids)
    place = jnp.concatenate(
        [
            (ids * 2 + x_hi) * CAP + slots_own,
            (across_ids * 2 + 1 - x_hi) * CAP + slots_across,
        ]
    ).reshape(2 * rows, TOP)
    resid, outgoing = residual_rows(y, core, terms, res_own, res_across, place.T)
    gate_other, up_other = flip_core(gate_own), flip_core(up_own)
    outgoing, gate_other, up_other = lax.optimization_barrier((outgoing, gate_other, up_other))
    arrived = lax.all_to_all(
        outgoing.reshape(NE, 2 * CAP, half), "exp", split_axis=0, concat_axis=0, tiled=True
    ).reshape(NE * 2 * CAP, half)
    down_other = flip_core(down_own)

    near, above, below, far = gather_y(arrived, 0)
    near_x = flip_x(near)
    above_x, below_x = from_y(near_x, 1), from_y(near_x, -1)
    far_x = flip_x(far)
    resid_across = flip_x(resid[rows:])
    gain = norm_gain.reshape(1, width)
    weights = (gate_own, gate_other, up_own, up_other)
    before = expert_in(x_hi[None], (near, above, below, far), gain, weights)
    *before, down_other = lax.optimization_barrier((*before, down_other))
    there = lax.dynamic_slice_in_dim(gain, (1 - x_hi) * half, half, 1)

    hidden, to_above, to_below, to_far = expert_rest(
        jnp.stack([1 - x_hi, x_hi]),
        (near_x, above_x, below_x, far_x),
        there,
        before,
        weights,
        down_own,
        down_other,
    )
    from_below = from_y(to_above, -1)
    from_above = from_y(to_below, 1)
    from_far = flip_x(to_far)
    above_lo, above_hi, below_lo, below_hi, cross, far_own, own = expert_out_part(
        hidden, down_own, down_other, ((0, 1), (0, 2), (1, 0), (0, 3), (0, 0)), (0, 1)
    )

    def added(*terms):
        return sum(t.astype(F32) for t in terms).astype(BF16)

    far_lo = from_y(added(far_own[:, :half], from_far[:, :half]), -1)
    far_hi = from_y(added(far_own[:, half:], from_far[:, half:]), 1)
    cross, above_hi, below_lo = lax.optimization_barrier(
        (added(cross, from_below, from_above), above_hi, below_lo)
    )
    from_cross = flip_x(cross)
    free_below = from_y(above_hi, -1)
    free_above = from_y(below_lo, 1)
    last_below = from_y(added(above_lo, far_lo), -1)
    last_above = from_y(added(below_hi, far_hi), 1)
    from_cross, last_below, last_above = lax.optimization_barrier(
        (from_cross, last_below, last_above)
    )
    expert_out = last_sum(own, from_cross, free_above, last_below, free_below, last_above)

    returned = lax.all_to_all(
        expert_out.reshape(NE, CAP, width), "exp", split_axis=0, concat_axis=0, tiled=True
    ).reshape(NE * CAP, width)
    route = jax.nn.softmax(route_logit, axis=1)
    position = (ids * CAP + slots_own).reshape(rows, TOP)
    column = jnp.arange(NE * CAP, dtype=jnp.int32)[None, :]
    halves = [resid[:rows], resid_across]
    own_row = jnp.where(
        x_hi == 0, jnp.concatenate(halves, 1), jnp.concatenate(halves[::-1], 1)
    ).astype(F32)
    for k in range(TOP):
        chosen = (position[:, k : k + 1] == column).astype(BF16)
        own_row = own_row + route[:, k : k + 1] * jnp.dot(
            chosen, returned, preferred_element_type=F32
        )
    return own_row.astype(BF16)


def solution(mesh):
    return jax.shard_map(
        per_device,
        mesh=mesh,
        in_specs=(
            P("ctx", "exp"),
            P("ctx", "exp"),
            P("ctx", "exp"),
            P("ctx", "exp", None),
            P("ctx"),
            P(("ctx", "exp"), None),
            P("exp", "ctx"),
            P(),
            P("exp", None, "ctx"),
            P("exp", None, "ctx"),
            P("exp", "ctx", None),
            P(("ctx", "exp"), None),
            P(("ctx", "exp"), None),
        ),
        out_specs=P(("ctx", "exp"), None),
        check_vma=False,
    )
```
